32 devices in a mesh: dp: 8 (over y, x, core), mp: 4 (over z).
Axes of the slice: x: 2, y: 2, z: 4, core: 2. Of those that a mesh axis runs over, the one named last changes fastest.
Arguments:
- tokens: bfloat16 [31360, 768], P(('dp', 'mp')), may hold values from -36 to 36
- cotangent: bfloat16 [31360, 768], P(('dp', 'mp')), may hold values from -5 to 5
- slot_live: int32 [8, 11], P('dp'), may hold values from 0 to 1, as said below
- vectors: float32 [6, 768], replicated, may hold values from -1.2 to 1.6, as said below
- vectors_momentum: float32 [6, 768], replicated, may hold values from -512 to 512
- vectors_average: float32 [6, 768], replicated, may hold values from -1.2 to 1.6, as said below
- column_bias: float32 [2, 768], P(None, 'mp'), may hold values from -1.75 to 1.75
- column_bias_momentum: float32 [2, 768], P(None, 'mp'), may hold values from -20480 to 20480
- column_bias_average: float32 [2, 768], P(None, 'mp'), may hold values from -1.75 to 1.75
- hidden_bias: float32 [3072], P('mp'), may hold values from -1.75 to 1.75
- hidden_bias_momentum: float32 [3072], P('mp'), may hold values from -320 to 320
- hidden_bias_average: float32 [3072], P('mp'), may hold values from -1.75 to 1.75
- attention_in: float32 [768, 3, 768], P('dp', None, 'mp'), may hold values from -0.21875 to 0.21875
- attention_in_momentum: float32 [768, 3, 768], P('dp', None, 'mp'), may hold values from -10240 to 10240
- attention_in_average: float32 [768, 3, 768], P('dp', None, 'mp'), may hold values from -0.21875 to 0.21875
- attention_out: float32 [768, 768], P('mp', 'dp'), may hold values from -3.5 to 3.5
- attention_out_momentum: float32 [768, 768], P('mp', 'dp'), may hold values from -56 to 56
- attention_out_average: float32 [768, 768], P('mp', 'dp'), may hold values from -3.5 to 3.5
- hidden_in: float32 [768, 3072], P('dp', 'mp'), may hold values from -0.21875 to 0.21875
- hidden_in_momentum: float32 [768, 3072], P('dp', 'mp'), may hold values from -256 to 256
- hidden_in_average: float32 [768, 3072], P('dp', 'mp'), may hold values from -0.21875 to 0.21875
- hidden_out: float32 [3072, 768], P('mp', 'dp'), may hold values from -0.109375 to 0.109375
- hidden_out_momentum: float32 [3072, 768], P('mp', 'dp'), may hold values from -512 to 512
- hidden_out_average: float32 [3072, 768], P('mp', 'dp'), may hold values from -0.109375 to 0.109375
Outputs:
- block_output: bfloat16 [31360, 768], P(('dp', 'mp'))
- input_gradient: bfloat16 [31360, 768], P(('dp', 'mp'))
- vectors_new: float32 [6, 768], replicated
- vectors_momentum_new: float32 [6, 768], replicated
- vectors_average_new: float32 [6, 768], replicated
- column_bias_new: float32 [2, 768], P(None, 'mp')
- column_bias_momentum_new: float32 [2, 768], P(None, 'mp')
- column_bias_average_new: float32 [2, 768], P(None, 'mp')
- hidden_bias_new: float32 [3072], P('mp')
- hidden_bias_momentum_new: float32 [3072], P('mp')
- hidden_bias_average_new: float32 [3072], P('mp')
- attention_in_new: float32 [768, 3, 768], P('dp', None, 'mp')
- attention_in_momentum_new: float32 [768, 3, 768], P('dp', None, 'mp')
- attention_in_average_new: float32 [768, 3, 768], P('dp', None, 'mp')
- attention_out_new: float32 [768, 768], P('mp', 'dp')
- attention_out_momentum_new: float32 [768, 768], P('mp', 'dp')
- attention_out_average_new: float32 [768, 768], P('mp', 'dp')
- hidden_in_new: float32 [768, 3072], P('dp', 'mp')
- hidden_in_momentum_new: float32 [768, 3072], P('dp', 'mp')
- hidden_in_average_new: float32 [768, 3072], P('dp', 'mp')
- hidden_out_new: float32 [3072, 768], P('mp', 'dp')
- hidden_out_momentum_new: float32 [3072, 768], P('mp', 'dp')
- hidden_out_average_new: float32 [3072, 768], P('mp', 'dp')
The draws below stay inside these ranges and needn't reach their ends.
Inputs may be any that keep to these rules, and one draw needn't show every extreme that they name: slot_live[g, s] is 1 where slot s of data group g holds an image and 0 where it is padding; in every draw some group has all 11 slots live. `vectors`: rows 0 and 2 are positive gains. `vectors_average`: rows 0 and 2 are positive.
All inputs are finite; a program needn't handle non-finite values.
Results may differ from the reference program's by a relative error of at most 0.017.
Values may be sent and summed in bfloat16 or wider, within the bound.
A program may use at most 192 MiB of HBM per device.

```python
import math
import jax
import jax.numpy as jnp
from jax import lax

MODEL_WIDTH = 768
HEADS = 12
HEAD_DIM = 64
FF = 3072
PATCH_L = 784
PATCH_S = 196
SLOT_L = 3
SLOT_S = 8
GROUPS = 8
SLOTS = 11
PATCH_ROWS_GROUP = 3920
ROWS = 31360
N_DP = 8
N_MP = 4


def draw_tokens(key, part):
    keys_four = jax.random.split(key, 3)
    row_scale = jnp.exp(jax.random.uniform(keys_four[0], (ROWS, 1), jnp.float32, -1.2, 1.2))
    col_scale = jnp.exp(jax.random.uniform(keys_four[1], (1, MODEL_WIDTH), jnp.float32, -1.2, 1.2))
    base_values = jnp.clip(jax.random.normal(keys_four[2], (ROWS, MODEL_WIDTH), jnp.float32), -4.0, 4.0)
    return jnp.clip(base_values * row_scale * col_scale, -36.0, 36.0).astype(jnp.bfloat16)


def vector_rows(key):
    keys_pair = jax.random.split(key, 2)
    gains = jnp.exp(jax.random.uniform(keys_pair[0], (2, MODEL_WIDTH), jnp.float32, -0.35, 0.35))
    shifts = jnp.clip(0.3 * jax.random.normal(keys_pair[1], (4, MODEL_WIDTH), jnp.float32), -1.2, 1.2)
    return jnp.stack([gains[0], shifts[0], gains[1], shifts[1], shifts[2], shifts[3]])


def draw_vectors(key, part):
    return vector_rows(jax.random.fold_in(key, 11))


def draw_vectors_average(key, part):
    return vector_rows(jax.random.fold_in(key, 12))


def draw_slot_live(key, part):
    keys_pair = jax.random.split(jax.random.fold_in(key, 13), 2)
    drawn = jax.random.randint(keys_pair[0], (GROUPS, SLOTS), 0, 10)
    filled = jax.random.randint(keys_pair[1], (), 0, GROUPS)
    chosen = jnp.arange(GROUPS, dtype=jnp.int32)[:, None] == filled
    return jnp.where(chosen, 1, jnp.where(drawn < 7, 1, 0)).astype(jnp.int32)


def strengthened(values, own_key, source, target, shards_of, factor):
    owner, partner = [(jnp.arange(values.shape[dim]) // (values.shape[dim] // shards_of)).reshape([-1 if axis == dim else 1 for axis in range(values.ndim)]) for dim in (source, target)]
    chosen = jax.random.permutation(own_key, shards_of)[partner]
    strong = (owner == chosen) | (owner == (partner + shards_of // 2) % shards_of)
    return jnp.where(strong, factor * values, values)


def levels(rng, shape, shards, low, largest):
    loudness = 1.0
    for dim, blocks in shards:
        heights = jax.random.uniform(jax.random.fold_in(jax.random.fold_in(rng, 6), dim), (blocks,), jnp.float32, low / len(shards), largest / len(shards))
        loudness = loudness * jnp.repeat(jnp.exp(heights), shape[dim] // blocks).reshape((-1,) + (1,) * (len(shape) - 1 - dim))
    return loudness


def bell_draw(key, dims, scale, limit, shards=(), kind=jnp.bfloat16):
    entries = jax.random.normal(key, dims, jnp.float32) * scale
    if len(shards) > 0:
        entries = levels(key, dims, shards, -0.22, 0.18) * entries
    return jnp.clip(entries, min=-limit, max=limit).astype(kind)


def noise_with(stream_key, extent, width, limit, shards, heavy, kind=jnp.bfloat16):
    result = width * jax.random.normal(stream_key, extent, jnp.float32)
    if shards:
        result = result * levels(stream_key, extent, shards, -0.22, 0.18)
    return jnp.clip(strengthened(result, jax.random.fold_in(stream_key, 3), *heavy), -limit, limit).astype(kind)


def setup_inputs(seed: int = 0) -> dict:
    arg_keys = jax.random.split(jax.random.key(seed), 25)
    return {
        "tokens": draw_tokens(jax.random.fold_in(arg_keys[24], 71), 0),
        "cotangent": noise_with(arg_keys[1], (ROWS, MODEL_WIDTH), 1.0, 5.0, ((0, 32),), (0, 1, 32, 2.75)),
        "slot_live": draw_slot_live(jax.random.fold_in(arg_keys[24], 71), 0),
        "vectors": draw_vectors(jax.random.fold_in(arg_keys[24], 71), 0),
        "vectors_momentum": bell_draw(arg_keys[4], (6, MODEL_WIDTH), (0.5 * ROWS ** 0.5), 512.0, (), jnp.float32),
        "vectors_average": draw_vectors_average(jax.random.fold_in(arg_keys[24], 71), 0),
        "column_bias": bell_draw(arg_keys[6], (2, MODEL_WIDTH), 0.3, 1.75, ((1, 4),), jnp.float32),
        "column_bias_momentum": bell_draw(arg_keys[7], (2, MODEL_WIDTH), (20.0 * ROWS ** 0.5), 20480.0, ((1, 4),), jnp.float32),
        "column_bias_average": bell_draw(arg_keys[8], (2, MODEL_WIDTH), 0.3, 1.75, ((1, 4),), jnp.float32),
        "hidden_bias": bell_draw(arg_keys[9], (FF,), 0.3, 1.75, ((0, 4),), jnp.float32),
        "hidden_bias_momentum": bell_draw(arg_keys[10], (FF,), (0.3 * ROWS ** 0.5), 320.0, ((0, 4),), jnp.float32),
        "hidden_bias_average": bell_draw(arg_keys[11], (FF,), 0.3, 1.75, ((0, 4),), jnp.float32),
        "attention_in": bell_draw(arg_keys[12], (MODEL_WIDTH, 3, MODEL_WIDTH), MODEL_WIDTH ** -0.5, 0.21875, ((0, 8), (2, 4)), jnp.float32),
        "attention_in_momentum": bell_draw(arg_keys[13], (MODEL_WIDTH, 3, MODEL_WIDTH), (10.0 * ROWS ** 0.5), 10240.0, ((0, 8), (2, 4)), jnp.float32),
        "attention_in_average": bell_draw(arg_keys[14], (MODEL_WIDTH, 3, MODEL_WIDTH), MODEL_WIDTH ** -0.5, 0.21875, ((0, 8), (2, 4)), jnp.float32),
        "attention_out": bell_draw(arg_keys[15], (MODEL_WIDTH, MODEL_WIDTH), (max(4 * MODEL_WIDTH // PATCH_L, 1)) ** -0.5, 3.5, ((0, 4), (1, 8)), jnp.float32),
        "attention_out_momentum": bell_draw(arg_keys[16], (MODEL_WIDTH, MODEL_WIDTH), (0.05 * ROWS ** 0.5), 56.0, ((0, 4), (1, 8)), jnp.float32),
        "attention_out_average": bell_draw(arg_keys[17], (MODEL_WIDTH, MODEL_WIDTH), (max(4 * MODEL_WIDTH // PATCH_L, 1)) ** -0.5, 3.5, ((0, 4), (1, 8)), jnp.float32),
        "hidden_in": bell_draw(arg_keys[18], (MODEL_WIDTH, FF), MODEL_WIDTH ** -0.5, 0.21875, ((0, 8), (1, 4)), jnp.float32),
        "hidden_in_momentum": bell_draw(arg_keys[19], (MODEL_WIDTH, FF), (0.25 * ROWS ** 0.5), 256.0, ((0, 8), (1, 4)), jnp.float32),
        "hidden_in_average": bell_draw(arg_keys[20], (MODEL_WIDTH, FF), MODEL_WIDTH ** -0.5, 0.21875, ((0, 8), (1, 4)), jnp.float32),
        "hidden_out": bell_draw(arg_keys[21], (FF, MODEL_WIDTH), FF ** -0.5, 0.109375, ((0, 4), (1, 8)), jnp.float32),
        "hidden_out_momentum": bell_draw(arg_keys[22], (FF, MODEL_WIDTH), (0.5 * ROWS ** 0.5), 512.0, ((0, 4), (1, 8)), jnp.float32),
        "hidden_out_average": bell_draw(arg_keys[23], (FF, MODEL_WIDTH), FF ** -0.5, 0.109375, ((0, 4), (1, 8)), jnp.float32),
    }


EPSILON = 1e-06
MOMENTUM = 0.9
AVERAGE = 0.8
DECAY = 0.0001
SQRT_HALF = 0.7071067811865476
RATE_VECTORS = 0.06
RATE_COLUMN = 0.01
RATE_HIDDEN = 0.4
RATE_ATTENTION_IN = 0.005
RATE_ATTENTION_OUT = 0.5
RATE_HIDDEN_IN = 0.05
RATE_HIDDEN_OUT = 0.015
TOP_PRECISION = lax.Precision.HIGHEST

@jax.custom_vjp
def reduced_copy(v):
    return lax.optimization_barrier(v.astype(jnp.bfloat16)).astype(jnp.float32)

@jax.custom_vjp
def low_back(v):
    return v

def low_keep(v):
    return (reduced_copy(v), None)

def low_pass(kept, grad):
    return (grad,)

def back_keep(v):
    return (v, None)

def back_low(kept, grad):
    return (reduced_copy(grad),)
reduced_copy.defvjp(low_keep, low_pass)
low_back.defvjp(back_keep, back_low)

def rounded_both(values):
    return low_back(reduced_copy(values))

def layer_norm(values, gain_row, shift_row):
    centre = lax.optimization_barrier(jnp.mean(values, axis=-1, keepdims=True))
    centred = values - centre
    spread = lax.optimization_barrier(jnp.mean(centred * centred, axis=-1, keepdims=True))
    return centred * lax.rsqrt(spread + EPSILON) * gain_row + shift_row

def gelu_exact(values):
    return 0.5 * values * (1.0 + lax.erf(values * SQRT_HALF))

def softmax_rows(scores):
    highest = lax.optimization_barrier(jnp.max(scores, axis=-1, keepdims=True))
    weights = jnp.exp(scores - highest)
    return weights / lax.optimization_barrier(jnp.sum(weights, axis=-1, keepdims=True))

def attend(queries, keys_in, values_in):
    factor = 1.0 / math.sqrt(HEAD_DIM)
    scores = low_back(factor * jnp.einsum('bqhe,bkhe->bhqk', queries, keys_in, precision=TOP_PRECISION))
    weights = reduced_copy(softmax_rows(scores))
    return jnp.einsum('bhqk,bkhe->bqhe', weights, values_in, precision=TOP_PRECISION)

def attend_single(blocks):
    return attend(blocks[0][None], blocks[1][None], blocks[2][None])[0]

def group_forward(rows_in, vectors, column_bias, hidden_bias, matrices):
    matrix_qkv, out_weight, up_weight, down_weight = matrices
    model_groups = N_MP
    head_columns = MODEL_WIDTH // model_groups
    hidden_columns = FF // model_groups
    boundary = SLOT_L * PATCH_L
    normed = reduced_copy(layer_norm(rows_in, vectors[0], vectors[1]))
    copies = low_back(jnp.broadcast_to(normed, (model_groups, PATCH_ROWS_GROUP, MODEL_WIDTH)))
    projected = jnp.einsum('mrd,dcmh->mrch', copies, matrix_qkv.reshape(MODEL_WIDTH, 3, model_groups, head_columns), precision=TOP_PRECISION)
    bias_rows = jnp.stack([column_bias[0], jnp.zeros_like(column_bias[0]), column_bias[1]]).reshape(3, model_groups, head_columns)
    projected = rounded_both(projected + jnp.transpose(bias_rows, (1, 0, 2))[:, None])
    heads_all = jnp.transpose(projected, (1, 2, 0, 3)).reshape(PATCH_ROWS_GROUP, 3, HEADS, HEAD_DIM)
    queries = heads_all[:, 0]
    keys_in = heads_all[:, 1]
    values_in = heads_all[:, 2]
    large_out = lax.map(jax.checkpoint(attend_single), (queries[:boundary].reshape(SLOT_L, PATCH_L, HEADS, HEAD_DIM), keys_in[:boundary].reshape(SLOT_L, PATCH_L, HEADS, HEAD_DIM), values_in[:boundary].reshape(SLOT_L, PATCH_L, HEADS, HEAD_DIM)))
    small_out = jax.checkpoint(attend)(queries[boundary:].reshape(SLOT_S, PATCH_S, HEADS, HEAD_DIM), keys_in[boundary:].reshape(SLOT_S, PATCH_S, HEADS, HEAD_DIM), values_in[boundary:].reshape(SLOT_S, PATCH_S, HEADS, HEAD_DIM))
    attention_result = rounded_both(jnp.concatenate([large_out.reshape(boundary, MODEL_WIDTH), small_out.reshape(PATCH_ROWS_GROUP - boundary, MODEL_WIDTH)], axis=0))
    attention_partial = reduced_copy(jnp.einsum('jtu,tun->tjn', attention_result.reshape(PATCH_ROWS_GROUP, model_groups, head_columns), out_weight.reshape(model_groups, head_columns, MODEL_WIDTH), precision=TOP_PRECISION))
    middle = rows_in + low_back(lax.optimization_barrier(jnp.sum(attention_partial, axis=0))) + vectors[4]
    normed_two = reduced_copy(layer_norm(middle, vectors[2], vectors[3]))
    second_replicas = low_back(jnp.broadcast_to(normed_two, (model_groups, PATCH_ROWS_GROUP, MODEL_WIDTH)))
    widened_copy = jnp.einsum('gtb,bgj->gtj', second_replicas, up_weight.reshape(MODEL_WIDTH, model_groups, hidden_columns), precision=TOP_PRECISION)
    widened_copy = widened_copy + hidden_bias.reshape(model_groups, 1, hidden_columns)
    gelu_hidden = reduced_copy(gelu_exact(low_back(widened_copy)))
    perceptron_partial = reduced_copy(jnp.einsum('unq,uqo->uno', gelu_hidden, down_weight.reshape(model_groups, hidden_columns, MODEL_WIDTH), precision=TOP_PRECISION))
    return middle + low_back(lax.optimization_barrier(jnp.sum(perceptron_partial, axis=0))) + vectors[5]

def forward(inputs, vectors, column_bias, hidden_bias, attention_in, attention_out, hidden_in, hidden_out):
    matrices = (reduced_copy(attention_in), reduced_copy(attention_out), reduced_copy(hidden_in), reduced_copy(hidden_out))
    groups_in = inputs.reshape(N_DP, PATCH_ROWS_GROUP, MODEL_WIDTH)

    def one_group(rows_in):
        return group_forward(rows_in, vectors, column_bias, hidden_bias, matrices)
    return lax.map(jax.checkpoint(one_group), groups_in).reshape(ROWS, MODEL_WIDTH)

def row_live(slot_live):
    position = jnp.arange(PATCH_ROWS_GROUP, dtype=jnp.int32)
    boundary = SLOT_L * PATCH_L
    slot_index = jnp.where(position < boundary, position // PATCH_L, SLOT_L + (position - boundary) // PATCH_S)
    matches = slot_index[:, None] == jnp.arange(SLOT_L + SLOT_S, dtype=jnp.int32)[None, :]
    return lax.optimization_barrier(jnp.sum(jnp.where(matches[None], slot_live[:, None, :], 0), axis=-1)).reshape(ROWS)

def nesterov(weight_old, moment_old, average_old, gradient, rate, decay):
    step_dir = gradient + decay * weight_old
    moment_new = MOMENTUM * moment_old + step_dir
    weight_new = weight_old - rate * (step_dir + MOMENTUM * moment_new)
    return (weight_new, moment_new, AVERAGE * average_old + (1.0 - AVERAGE) * weight_new)

def reference(tokens, cotangent, slot_live, vectors, vectors_momentum, vectors_average, column_bias, column_bias_momentum, column_bias_average, hidden_bias, hidden_bias_momentum, hidden_bias_average, attention_in, attention_in_momentum, attention_in_average, attention_out, attention_out_momentum, attention_out_average, hidden_in, hidden_in_momentum, hidden_in_average, hidden_out, hidden_out_momentum, hidden_out_average):
    live_rows = row_live(slot_live).astype(jnp.float32)
    inputs = tokens.astype(jnp.float32)
    output, pull_back = jax.vjp(forward, inputs, vectors, column_bias, hidden_bias, attention_in, attention_out, hidden_in, hidden_out)
    grads_all = pull_back(cotangent.astype(jnp.float32) * live_rows[:, None])
    root_rows = math.sqrt(ROWS)
    vectors_new, vectors_moment, vectors_mean = nesterov(vectors, vectors_momentum, vectors_average, grads_all[1], RATE_VECTORS / root_rows, 0.0)
    column_new, column_moment, column_mean = nesterov(column_bias, column_bias_momentum, column_bias_average, grads_all[2], RATE_COLUMN / root_rows, 0.0)
    hidden_new, hidden_moment, hidden_mean = nesterov(hidden_bias, hidden_bias_momentum, hidden_bias_average, grads_all[3], RATE_HIDDEN / root_rows, 0.0)
    qkv_new, qkv_moment, qkv_mean = nesterov(attention_in, attention_in_momentum, attention_in_average, grads_all[4], RATE_ATTENTION_IN / root_rows, DECAY)
    outer_new, outer_moment, outer_mean = nesterov(attention_out, attention_out_momentum, attention_out_average, grads_all[5], RATE_ATTENTION_OUT / root_rows, DECAY)
    upper_new, upper_moment, upper_mean = nesterov(hidden_in, hidden_in_momentum, hidden_in_average, grads_all[6], RATE_HIDDEN_IN / root_rows, DECAY)
    lower_new, lower_moment, lower_mean = nesterov(hidden_out, hidden_out_momentum, hidden_out_average, grads_all[7], RATE_HIDDEN_OUT / root_rows, DECAY)
    return (output.astype(jnp.bfloat16), grads_all[0].astype(jnp.bfloat16), vectors_new, vectors_moment, vectors_mean, column_new, column_moment, column_mean, hidden_new, hidden_moment, hidden_mean, qkv_new, qkv_moment, qkv_mean, outer_new, outer_moment, outer_mean, upper_new, upper_moment, upper_mean, lower_new, lower_moment, lower_mean)
```

```python
import functools
import math

import jax
import jax.numpy as jnp
from jax import lax
from jax.experimental import pallas as pl
from jax.experimental.pallas import tpu as pltpu
from jax.sharding import PartitionSpec as P

F32, BF16 = jnp.float32, jnp.bfloat16
WIDTH = 768
HEAD_DIM = 64
PATCH_L = 784
PATCH_S = 196
SLOT_L = 3
SLOT_S = 8
UNIT = 196
ROWS = 208
UNITS = 8
BLOCK = 4 * ROWS
PAIRS = 6
CHUNKS = 3
COLS = 2304

EPSILON = 1e-06
MOMENTUM = 0.9
AVERAGE = 0.8
DECAY = 0.0001
RATE_VECTORS = 0.06
RATE_COLUMN = 0.01
RATE_HIDDEN = 0.4
RATE_ATTENTION_IN = 0.005
RATE_ATTENTION_OUT = 0.5
RATE_HIDDEN_IN = 0.05
RATE_HIDDEN_OUT = 0.015


def nn(a, b):
    return lax.dot_general(a, b, (((1,), (0,)), ((), ())), preferred_element_type=F32)


def nt(a, b):
    return lax.dot_general(a, b, (((1,), (1,)), ((), ())), preferred_element_type=F32)


def tn(a, b):
    return lax.dot_general(a, b, (((0,), (0,)), ((), ())), preferred_element_type=F32)


def normalize(values):
    centred = values - jnp.mean(values, axis=-1, keepdims=True)
    spread = jnp.mean(centred * centred, axis=-1, keepdims=True)
    scale = lax.rsqrt(spread + EPSILON)
    return centred * scale, scale


def norm_back(cotangent, gain, n, scale):
    cg = cotangent * gain
    return scale * (
        cg - jnp.mean(cg, axis=-1, keepdims=True) - n * jnp.mean(cg * n, axis=-1, keepdims=True)
    )


def column_sums(values):
    return jnp.sum(values, axis=0, keepdims=True)


def split_three(column):
    high = column.astype(BF16)
    rest = column - high.astype(F32)
    mid = rest.astype(BF16)
    low = (rest - mid.astype(F32)).astype(BF16)
    return high, mid, low


def gelu_terms(u):
    e = jnp.exp(u * u * -0.5)
    k = 1.0 / (1.0 + jnp.abs(u) * (0.3275911 * math.sqrt(0.5)))
    poly = k * (
        0.5 * 0.254829592
        + k * (0.5 * -0.284496736 + k * (0.5 * 1.421413741 + k * (0.5 * -1.453152027 + k * (0.5 * 1.061405429))))
    )
    tail = poly * e
    big_phi = jnp.where(u < 0.0, tail, 1.0 - tail)
    return big_phi, u * e * (1.0 / math.sqrt(2.0 * math.pi))


def block_of(ref, b):
    return ref[pl.ds(4 * b, 4)].reshape(BLOCK, ref.shape[-1])


def put_block(ref, b, value):
    ref[pl.ds(4 * b, 4)] = value.reshape(4, ROWS, value.shape[-1])


def lanes():
    return lax.broadcasted_iota(jnp.int32, (1, 128), 1)


def pad_bias(rows):
    at = lax.broadcasted_iota(jnp.int32, (rows, 1), 0)
    return jnp.where(lax.rem(at, ROWS) >= UNIT, -1e30, 0.0).astype(F32)


def masks(h):
    lane = lanes()
    own = (lane < 64) if h == 0 else (lane >= 64)
    first = 64 if h == 0 else 0
    return lane, own, first


def extend_keys(k, h, pad):
    lane, own, first = masks(h)
    ext = jnp.where(lane == first, pad, jnp.where((lane > first) & (lane < first + 4), 1.0, 0.0))
    return jnp.where(own, k.astype(F32), ext).astype(BF16)


def extend_queries(q, h, column=None):
    lane, own, first = masks(h)
    ext = jnp.where(lane == first, 1.0, 0.0).astype(F32)
    if column is not None:
        for i, part in enumerate(split_three(-column)):
            ext = jnp.where(lane == first + 1 + i, part.astype(F32), ext)
    return jnp.where(own, q.astype(F32), ext).astype(BF16)


def extend_grads(g, h, column):
    lane, own, first = masks(h)
    ext = jnp.zeros((1, 128), F32)
    for i, part in enumerate(split_three(-column)):
        ext = jnp.where(lane == first + 1 + i, part.astype(F32), ext)
    return jnp.where(own, g.astype(F32), ext).astype(BF16)


def extend_values(v, h):
    lane, own, first = masks(h)
    ext = jnp.where((lane > first) & (lane < first + 4), 1.0, 0.0)
    return jnp.where(own, v.astype(F32), ext).astype(BF16)


def attend_pair(q, k, v, pad):
    outs, logs = [], []
    for h in (0, 1):
        s = nt(extend_queries(q, h), extend_keys(k, h, pad))
        top = jnp.max(s, axis=-1, keepdims=True)
        e = jnp.exp(s - top)
        total = jnp.sum(e, axis=-1, keepdims=True)
        outs.append(nn(e.astype(BF16), v) * (1.0 / total))
        logs.append(top + jnp.log(total))
    return jnp.where(lanes() < 64, outs[0], outs[1]).astype(BF16), logs


def attend_pair_back(q, k, v, g, logs, dots, pad):
    dq, dk, dv = [], [], []
    for h in (0, 1):
        p = jnp.exp(nt(extend_queries(q, h, logs[h]), extend_keys(k, h, pad)))
        dp = nt(extend_grads(g, h, dots[h]), extend_values(v, h))
        ds = (p * dp).astype(BF16)
        dv.append(tn(p.astype(BF16), g))
        dq.append(nn(ds, k))
        dk.append(tn(ds, q))
    left = lanes() < 64
    return [jnp.where(left, t[0], t[1]).astype(BF16) for t in (dq, dk, dv)]


def lane_column(values, lane):
    return jnp.sum(jnp.where(lanes() == lane, values, 0.0), axis=-1, keepdims=True)


def kernel(
    x_ref, dy_in, g_in, vec_ref, qb_ref, hb_ref,
    yout, gin, gout, small_ref, six_ref,
    g, wb, qkv, att, h2, dy, y, e, lse, zdu, sem,
):
    rank = lax.axis_index("mp")
    large = rank < 3
    blocks = jnp.where(large, 1, 2)
    vrow = lambda i: vec_ref[i : i + 1, :]

    copies = [pltpu.make_async_copy(g_in, g, sem.at[0]), pltpu.make_async_copy(dy_in, dy, sem.at[1])]
    for c in copies:
        c.start()
    for c in copies:
        c.wait()
    small_ref[...] = jnp.zeros_like(small_ref)
    six_ref[...] = jnp.zeros_like(six_ref)

    def unpack_b():
        parts = [g[z, :, 384:768] for z in range(4)]
        o01 = [t[:, 0:128] for t in parts]
        qs, ks, vs, o2 = ([t[:, 128 + 64 * i : 192 + 64 * i] for t in parts] for i in range(4))
        cat = lambda a, b: jnp.concatenate([a, b], axis=1)
        cols = []
        for i in (0, 2):
            cols += [cat(qs[i], qs[i + 1]), cat(ks[i], ks[i + 1]), cat(vs[i], vs[i + 1])]
        cols += o01 + [cat(o2[0], o2[1]), cat(o2[2], o2[3])]
        for i, t in enumerate(cols):
            wb[:, 128 * i : 128 * (i + 1)] = t

    unpack_b()

    def w_pair(i):
        if i < 2:
            return jnp.concatenate([g[2 * i, :, 0:384], g[2 * i + 1, :, 0:384]], axis=1)
        return wb[:, 0:768]

    @pl.loop(0, blocks)
    def _(b):
        n, _s = normalize(block_of(x_ref, b).astype(F32))
        h1 = (n * vrow(0) + vrow(1)).astype(BF16)
        for i in range(3):
            out = nn(h1, w_pair(i)) + qb_ref[:, 768 * i : 768 * (i + 1)]
            qkv[pl.ds(4 * b, 4), :, 768 * i : 768 * (i + 1)] = out.astype(BF16).reshape(4, ROWS, 768)

    def pair_columns(ref, u0, count, p):
        return [
            ref[pl.ds(u0, count), :, pl.ds(pl.multiple_of(384 * p + 128 * i, 128), 128)].reshape(count * ROWS, 128)
            for i in range(3)
        ]

    def forward_image(u0, count, p):
        q, k, v = pair_columns(qkv, u0, count, p)
        out, logs = attend_pair(q, k, v, pad_bias(count * ROWS))
        att[pl.ds(u0, count), :, pl.ds(pl.multiple_of(128 * p, 128), 128)] = out.reshape(count, ROWS, 128)
        old = lse[pl.ds(u0, count)].reshape(count * ROWS, 128)
        for h in (0, 1):
            old = jnp.where(lanes() == 2 * p + h, logs[h], old)
        lse[pl.ds(u0, count)] = old.reshape(count, ROWS, 128)

    @pl.when(large)
    def _():
        pl.loop(0, PAIRS)(lambda p: forward_image(0, 4, p))

    @pl.when(jnp.logical_not(large))
    def _():
        @pl.loop(0, UNITS)
        def _(u):
            for p in range(PAIRS):
                forward_image(u, 1, p)

    def middle_of(b):
        return block_of(x_ref, b).astype(F32) + nt(block_of(att, b), wb[:, 768:1536]) + vrow(4)

    @pl.loop(0, blocks)
    def _(b):
        mid = middle_of(b)
        n, _s = normalize(mid)
        put_block(h2, b, (n * vrow(2) + vrow(3)).astype(BF16))
        put_block(y, b, mid + vrow(5))
        put_block(e, b, jnp.zeros((BLOCK, WIDTH), F32))

    @pl.loop(0, 2 * CHUNKS)
    def _(s):
        c, zp = s // 2, s % 2
        at = pl.multiple_of(768 + 512 * c, 128)
        up = jnp.concatenate([g[2 * zp, :, pl.ds(at, 256)], g[2 * zp + 1, :, pl.ds(at, 256)]], axis=1)
        at2 = pl.multiple_of(at + 256, 128)
        down = jnp.concatenate([g[2 * zp, :, pl.ds(at2, 256)], g[2 * zp + 1, :, pl.ds(at2, 256)]], axis=1)
        hb = hb_ref[pl.ds(s, 1), :]

        @pl.loop(0, blocks)
        def _(b):
            u = nn(block_of(h2, b), up) + hb
            dz = nn(block_of(dy, b), down)
            big_phi, small_phi = gelu_terms(u)
            z = (u * big_phi).astype(BF16)
            du = (dz * (big_phi + small_phi)).astype(BF16)
            zdu[pl.ds(4 * b, 4), :, 0:512] = z.reshape(4, ROWS, 512)
            zdu[pl.ds(4 * b, 4), :, 512:1024] = du.reshape(4, ROWS, 512)
            six_ref[s, 0:1, :] += column_sums(du.astype(F32))
            put_block(y, b, block_of(y, b) + nt(z, down))
            put_block(e, b, block_of(e, b) + nt(du, up))

        def grads(count):
            rows = count * ROWS
            h2v, dyv = h2[0:count].reshape(rows, WIDTH), dy[0:count].reshape(rows, WIDTH)
            gu = tn(h2v, zdu[0:count, :, 512:1024].reshape(rows, 512)).astype(BF16)
            gd = tn(dyv, zdu[0:count, :, 0:512].reshape(rows, 512)).astype(BF16)
            for i in range(2):
                g[2 * zp + i, :, pl.ds(at, 256)] = gu[:, 256 * i : 256 * (i + 1)]
                g[2 * zp + i, :, pl.ds(at2, 256)] = gd[:, 256 * i : 256 * (i + 1)]

        pl.when(large)(lambda: grads(4))
        pl.when(jnp.logical_not(large))(lambda: grads(8))

    @pl.loop(0, blocks)
    def _(b):
        zdu[pl.ds(4 * b, 4), :, 0:768] = block_of(y, b).astype(BF16).reshape(4, ROWS, WIDTH)
        n, scale = normalize(middle_of(b))
        grad = block_of(e, b)
        dyv = block_of(dy, b).astype(F32)
        dmid = dyv + norm_back(grad, vrow(2), n, scale)
        small_ref[2:3, :] += column_sums(grad * n)
        small_ref[3:4, :] += column_sums(grad)
        small_ref[4:5, :] += column_sums(dmid)
        small_ref[5:6, :] += column_sums(dyv)
        put_block(e, b, dmid)
        put_block(h2, b, dmid.astype(BF16))

    out_copy = pltpu.make_async_copy(zdu.at[:, :, 0:768], yout, sem.at[0])
    out_copy.start()

    def out_grads(count):
        rows = count * ROWS
        go = tn(h2[0:count].reshape(rows, WIDTH), att[0:count].reshape(rows, WIDTH)).astype(BF16)
        for z in range(4):
            g[z, :, 384:512] = go[:, 128 * z : 128 * (z + 1)]
            g[z, :, 704:768] = go[:, 512 + 64 * z : 576 + 64 * z]

    pl.when(large)(lambda: out_grads(4))
    pl.when(jnp.logical_not(large))(lambda: out_grads(8))

    @pl.loop(0, blocks)
    def _(b):
        put_block(dy, b, nn(block_of(h2, b), wb[:, 768:1536]).astype(BF16))

    def backward_image(u0, count, p):
        rows = count * ROWS
        q, k, v = pair_columns(qkv, u0, count, p)
        at = pl.multiple_of(128 * p, 128)
        grad = dy[pl.ds(u0, count), :, pl.ds(at, 128)].reshape(rows, 128)
        out = att[pl.ds(u0, count), :, pl.ds(at, 128)].reshape(rows, 128)
        prod = grad.astype(F32) * out.astype(F32)
        left = lanes() < 64
        dots = [
            jnp.sum(jnp.where(left, prod, 0.0), axis=-1, keepdims=True),
            jnp.sum(jnp.where(left, 0.0, prod), axis=-1, keepdims=True),
        ]
        all_logs = lse[pl.ds(u0, count)].reshape(rows, 128)
        logs = [lane_column(all_logs, 2 * p + h) for h in (0, 1)]
        parts = attend_pair_back(q, k, v, grad, logs, dots, pad_bias(rows))
        for i, part in enumerate(parts):
            qkv[pl.ds(u0, count), :, pl.ds(pl.multiple_of(384 * p + 128 * i, 128), 128)] = part.reshape(count, ROWS, 128)
        six_ref[p, 1:2, 0:128] += column_sums(parts[0].astype(F32))
        six_ref[p, 1:2, 128:256] += column_sums(parts[2].astype(F32))

    @pl.when(large)
    def _():
        pl.loop(0, PAIRS)(lambda p: backward_image(0, 4, p))

    @pl.when(jnp.logical_not(large))
    def _():
        @pl.loop(0, UNITS)
        def _(u):
            for p in range(PAIRS):
                backward_image(u, 1, p)

    out_copy.wait()

    @pl.loop(0, blocks)
    def _(b):
        n, scale = normalize(block_of(x_ref, b).astype(F32))
        put_block(h2, b, (n * vrow(0) + vrow(1)).astype(BF16))
        grad = nt(block_of(qkv, b)[:, 0:768], w_pair(0))
        grad += nt(block_of(qkv, b)[:, 768:1536], w_pair(1))
        grad += nt(block_of(qkv, b)[:, 1536:2304], w_pair(2))
        small_ref[0:1, :] += column_sums(grad * n)
        small_ref[1:2, :] += column_sums(grad)
        out = block_of(e, b) + norm_back(grad, vrow(0), n, scale)
        zdu[pl.ds(4 * b, 4), :, 0:768] = out.astype(BF16).reshape(4, ROWS, WIDTH)

    in_copy = pltpu.make_async_copy(zdu.at[:, :, 0:768], gin, sem.at[0])
    in_copy.start()

    def in_grads(count):
        rows = count * ROWS
        h1 = h2[0:count].reshape(rows, WIDTH)
        for i in range(3):
            gq = tn(h1, qkv[0:count, :, 768 * i : 768 * (i + 1)].reshape(rows, 768)).astype(BF16)
            if i < 2:
                g[2 * i, :, 0:384] = gq[:, 0:384]
                g[2 * i + 1, :, 0:384] = gq[:, 384:768]
            else:
                for z in range(4):
                    base = 384 * (z // 2) + 64 * (z % 2)
                    for t in range(3):
                        g[z, :, 512 + 64 * t : 576 + 64 * t] = gq[:, base + 128 * t : base + 128 * t + 64]

    pl.when(large)(lambda: in_grads(4))
    pl.when(jnp.logical_not(large))(lambda: in_grads(8))

    g_copy = pltpu.make_async_copy(g, gout, sem.at[1])
    g_copy.start()
    in_copy.wait()
    g_copy.wait()


def run_kernel(x, dy, weights, vectors, qkv_bias, hidden_rows):
    vmem, hbm = pl.BlockSpec(memory_space=pltpu.VMEM), pl.BlockSpec(memory_space=pl.ANY)
    units = (UNITS, ROWS, WIDTH)
    return pl.pallas_call(
        kernel,
        out_shape=[
            jax.ShapeDtypeStruct(units, BF16),
            jax.ShapeDtypeStruct(units, BF16),
            jax.ShapeDtypeStruct((4, WIDTH, COLS), BF16),
            jax.ShapeDtypeStruct((8, 768), F32),
            jax.ShapeDtypeStruct((6, 8, 512), F32),
        ],
        in_specs=[vmem, hbm, hbm, vmem, vmem, vmem],
        out_specs=[hbm, hbm, hbm, vmem, vmem],
        scratch_shapes=[
            pltpu.VMEM((4, WIDTH, COLS), BF16),
            pltpu.VMEM((WIDTH, 1536), BF16),
            pltpu.VMEM((UNITS, ROWS, COLS), BF16),
            pltpu.VMEM(units, BF16),
            pltpu.VMEM(units, BF16),
            pltpu.VMEM(units, BF16),
            pltpu.VMEM(units, F32),
            pltpu.VMEM(units, F32),
            pltpu.VMEM((UNITS, ROWS, 128), F32),
            pltpu.VMEM((UNITS, ROWS, 1024), BF16),
            pltpu.SemaphoreType.DMA((2,)),
        ],
        compiler_params=pltpu.CompilerParams(vmem_limit_bytes=64 * 2**20 - 2**16),
    )(x, dy, weights, vectors, qkv_bias, hidden_rows)


def pack_shard(attention_in, attention_out, hidden_in, hidden_out):
    q, k, v = attention_in[:, 0] * 0.125, attention_in[:, 1], attention_in[:, 2]
    out_t, down_t = attention_out.T, hidden_out.T
    cols = [q[:, :128], k[:, :128], v[:, :128], out_t[:, :128], q[:, 128:], k[:, 128:], v[:, 128:], out_t[:, 128:]]
    for c in range(CHUNKS):
        cols += [hidden_in[:, 256 * c : 256 * (c + 1)], down_t[:, 256 * c : 256 * (c + 1)]]
    return jnp.concatenate([t.astype(BF16) for t in cols], axis=1)


def unpack_shard(grad):
    q = jnp.concatenate([grad[:, 0:128], grad[:, 512:576]], axis=1) * 0.125
    k = jnp.concatenate([grad[:, 128:256], grad[:, 576:640]], axis=1)
    v = jnp.concatenate([grad[:, 256:384], grad[:, 640:704]], axis=1)
    out_t = jnp.concatenate([grad[:, 384:512], grad[:, 704:768]], axis=1)
    up = jnp.concatenate([grad[:, 768 + 512 * c : 1024 + 512 * c] for c in range(CHUNKS)], axis=1)
    down = jnp.concatenate([grad[:, 1024 + 512 * c : 1280 + 512 * c] for c in range(CHUNKS)], axis=1)
    return jnp.stack([q, k, v], axis=1), out_t.T, up, down.T


def nesterov(weight_old, moment_old, average_old, gradient, rate, decay):
    step_dir = gradient + decay * weight_old
    moment_new = MOMENTUM * moment_old + step_dir
    weight_new = weight_old - rate * (step_dir + MOMENTUM * moment_new)
    return (weight_new, moment_new, AVERAGE * average_old + (1.0 - AVERAGE) * weight_new)


def pair_order(blocks):
    first = [blocks[z, 0:2].reshape(128) for z in range(4)]
    return first + [blocks[0:2, 2].reshape(128), blocks[2:4, 2].reshape(128)]


def local(
    tokens, cotangent, slot_live,
    vectors, vectors_momentum, vectors_average,
    column_bias, column_bias_momentum, column_bias_average,
    hidden_bias, hidden_bias_momentum, hidden_bias_average,
    attention_in, attention_in_momentum, attention_in_average,
    attention_out, attention_out_momentum, attention_out_average,
    hidden_in, hidden_in_momentum, hidden_in_average,
    hidden_out, hidden_out_momentum, hidden_out_average,
):
    rows_dev = tokens.shape[0]
    rank = lax.axis_index("mp")
    total_rows = rows_dev * lax.axis_size("mp") * lax.axis_size("dp")
    own_units = rows_dev // UNIT
    unit = rank * own_units + jnp.arange(own_units, dtype=jnp.int32)
    slot = jnp.where(unit < 4 * SLOT_L, unit // 4, unit - 3 * SLOT_L)
    live = jnp.sum(
        jnp.where(slot[:, None] == jnp.arange(slot_live.shape[1], dtype=jnp.int32)[None], slot_live, 0), axis=1
    ).astype(BF16)

    def in_units(rows):
        return jnp.pad(rows.reshape(own_units, UNIT, WIDTH), ((0, 0), (0, ROWS - UNIT), (0, 0)))

    def to_work(units):
        got = lax.ppermute(units[2:5], "mp", [(0, 1), (1, 2), (2, 3)])
        row = jnp.concatenate([got, units, jnp.zeros((3, ROWS, WIDTH), BF16)], axis=0)
        return lax.dynamic_slice_in_dim(row, 3 - rank, UNITS, 0)

    def from_work(work):
        got = lax.ppermute(work[0:3], "mp", [(1, 0), (2, 1), (3, 2)])
        index = jnp.arange(own_units, dtype=jnp.int32)
        row = jnp.concatenate([work, got], axis=0)
        pick = jnp.where((rank == 3) | (index < 4 - rank), rank + index, 8 + index - (4 - rank))
        units = jnp.take(row, pick, axis=0)
        return units[:, :UNIT].reshape(rows_dev, WIDTH)

    x = to_work(in_units(tokens))
    dy = to_work(in_units(cotangent) * live[:, None, None])
    shard = pack_shard(attention_in, attention_out, hidden_in, hidden_out)
    weights = lax.all_gather(lax.all_gather(shard, "dp", axis=0, tiled=True), "mp", axis=0)
    cb = lax.all_gather(column_bias, "mp", axis=0)
    bq, bv = pair_order(cb[:, 0].reshape(4, 3, 64) * 0.125), pair_order(cb[:, 1].reshape(4, 3, 64))
    qkv_bias = jnp.concatenate([t for p in range(PAIRS) for t in (bq[p], jnp.zeros((128,), F32), bv[p])])[None]
    hb = lax.all_gather(hidden_bias, "mp", axis=0)
    hidden_rows = jnp.transpose(hb.reshape(2, 2, CHUNKS, 256), (2, 0, 1, 3)).reshape(2 * CHUNKS, 512)

    yout, gin, grads, small, six = run_kernel(x, dy, weights, vectors, qkv_bias, hidden_rows)
    block_output, input_gradient = from_work(yout), from_work(gin)
    reduced = lax.psum_scatter(grads, "mp", scatter_dimension=0, tiled=True)[0]
    reduced = lax.psum_scatter(reduced, "dp", scatter_dimension=0, tiled=True).astype(F32)
    small, six = lax.psum((small, six), ("dp", "mp"))
    vector_grad = small[0:6]
    hidden_grad = jnp.transpose(six[:, 0].reshape(CHUNKS, 2, 2, 256), (1, 2, 0, 3)).reshape(4, 768)
    hidden_grad = lax.dynamic_index_in_dim(hidden_grad, rank, 0, keepdims=False)
    pq, pv = six[:, 1, 0:128].reshape(PAIRS, 2, 64), six[:, 1, 128:256].reshape(PAIRS, 2, 64)

    def own_heads(pairs):
        second = pairs[4:6].reshape(4, 64)
        return jnp.concatenate(
            [lax.dynamic_index_in_dim(pairs, rank, 0, keepdims=False).reshape(128),
             lax.dynamic_index_in_dim(second, rank, 0, keepdims=False)]
        )

    column_grad = jnp.stack([own_heads(pq) * 0.125, own_heads(pv)])
    gqkv, gout, gup, gdown = unpack_shard(reduced)
    root = math.sqrt(total_rows)
    steps = (
        (vectors, vectors_momentum, vectors_average, vector_grad, RATE_VECTORS, 0.0),
        (column_bias, column_bias_momentum, column_bias_average, column_grad, RATE_COLUMN, 0.0),
        (hidden_bias, hidden_bias_momentum, hidden_bias_average, hidden_grad, RATE_HIDDEN, 0.0),
        (attention_in, attention_in_momentum, attention_in_average, gqkv, RATE_ATTENTION_IN, DECAY),
        (attention_out, attention_out_momentum, attention_out_average, gout, RATE_ATTENTION_OUT, DECAY),
        (hidden_in, hidden_in_momentum, hidden_in_average, gup, RATE_HIDDEN_IN, DECAY),
        (hidden_out, hidden_out_momentum, hidden_out_average, gdown, RATE_HIDDEN_OUT, DECAY),
    )
    outs = [block_output, input_gradient]
    for weight, moment, average, gradient, rate, decay in steps:
        outs.extend(nesterov(weight, moment, average, gradient, rate / root, decay))
    return tuple(outs)


def solution(mesh):
    rows, matrix, side = P(("dp", "mp"), None), P("dp", None, "mp"), P("mp", "dp")
    params = [P()] * 3 + [P(None, "mp")] * 3 + [P("mp")] * 3 + [matrix] * 3 + [side] * 3 + [P("dp", "mp")] * 3 + [side] * 3
    return jax.shard_map(
        local,
        mesh=mesh,
        in_specs=(rows, rows, P("dp", None), *params),
        out_specs=(rows, rows, *params),
        check_vma=False,
    )
```

```python
import functools
import math
import types

import jax
import jax.numpy as jnp
from jax import lax
from jax.experimental import pallas as pl
from jax.experimental.pallas import tpu as pltpu
from jax.sharding import PartitionSpec as P

F32, BF16 = jnp.float32, jnp.bfloat16
WIDTH = 768
HEAD_DIM = 64
PATCH_L = 784
PATCH_S = 196
SLOT_L = 3
SLOT_S = 8
UNIT = 196
ROWS = 208
UNITS = 8
BLOCK = 4 * ROWS
PAIRS = 6
CHUNKS = 3
COLS = 2304

EPSILON = 1e-06
MOMENTUM = 0.9
AVERAGE = 0.8
DECAY = 0.0001
RATE_VECTORS = 0.06
RATE_COLUMN = 0.01
RATE_HIDDEN = 0.4
RATE_ATTENTION_IN = 0.005
RATE_ATTENTION_OUT = 0.5
RATE_HIDDEN_IN = 0.05
RATE_HIDDEN_OUT = 0.015


def nn(a, b):
    return lax.dot_general(a, b, (((1,), (0,)), ((), ())), preferred_element_type=F32)


def nt(a, b):
    return lax.dot_general(a, b, (((1,), (1,)), ((), ())), preferred_element_type=F32)


def tn(a, b):
    return lax.dot_general(a, b, (((0,), (0,)), ((), ())), preferred_element_type=F32)


def normalize(values):
    centred = values - jnp.mean(values, axis=-1, keepdims=True)
    spread = jnp.mean(centred * centred, axis=-1, keepdims=True)
    scale = lax.rsqrt(spread + EPSILON)
    return centred * scale, scale


def norm_back(cotangent, gain, n, scale):
    cg = cotangent * gain
    return scale * (
        cg - jnp.mean(cg, axis=-1, keepdims=True) - n * jnp.mean(cg * n, axis=-1, keepdims=True)
    )


def column_sums(values):
    return jnp.sum(values, axis=0, keepdims=True)


def split_three(values):
    high = values.astype(BF16).astype(F32)
    mid = (values - high).astype(BF16).astype(F32)
    return high, mid, values - high - mid


def gelu_terms(u):
    e = jnp.exp(u * u * -0.5)
    k = 1.0 / (1.0 + jnp.abs(u) * (0.3275911 * math.sqrt(0.5)))
    poly = k * (
        0.5 * 0.254829592
        + k * (0.5 * -0.284496736 + k * (0.5 * 1.421413741 + k * (0.5 * -1.453152027 + k * (0.5 * 1.061405429))))
    )
    tail = poly * e
    big_phi = jnp.where(u < 0.0, tail, 1.0 - tail)
    return big_phi, u * e * (1.0 / math.sqrt(2.0 * math.pi))


def block_of(ref, b):
    return ref[pl.ds(4 * b, 4)].reshape(BLOCK, ref.shape[-1])


def put_block(ref, b, value):
    ref[pl.ds(4 * b, 4)] = value.reshape(4, ROWS, value.shape[-1])


def lanes():
    return lax.broadcasted_iota(jnp.int32, (1, 128), 1)


def pad_lane(rows):
    at = lax.broadcasted_iota(jnp.int32, (rows, 128), 0)
    lane = lax.broadcasted_iota(jnp.int32, (rows, 128), 1)
    return jnp.where((lax.rem(at, ROWS) >= UNIT) & (lane == 127), -1e30, 0.0).astype(BF16)


def own_lanes(values, h):
    mask = jnp.where((lanes() < 64) == (h == 0), 1.0, 0.0).astype(BF16)
    return values * mask


def cat(*parts):
    return jnp.concatenate(parts, axis=1)


def one_lanes(*which):
    hit = functools.reduce(jnp.logical_or, [lanes() == w for w in which])
    return jnp.where(hit, 1.0, 0.0).astype(BF16)


def attend_pair(q, k, v, pad, splits):
    rows = q.shape[0]
    part = rows // splits
    keys = cat(k, pad)
    ones = jnp.broadcast_to(one_lanes(127), (part, 128))
    outs, logs = [], [[], []]
    for i in range(splits):
        both = []
        for h in (0, 1):
            s = nt(cat(own_lanes(q[i * part : (i + 1) * part], h), ones), keys)
            top = jnp.max(s, axis=-1, keepdims=True)
            e = jnp.exp(s - top)
            total = jnp.sum(e, axis=-1, keepdims=True)
            both.append(nn(e.astype(BF16), v) * (1.0 / total))
            logs[h].append(top + jnp.log(total))
        outs.append(jnp.where(lanes() < 64, both[0], both[1]).astype(BF16))
    join = lambda t: t[0] if len(t) == 1 else jnp.concatenate(t, axis=0)
    return join(outs), [join(t) for t in logs]


def attend_pair_back(q, k, v, g, terms, first_head, pad, splits):
    rows = q.shape[0]
    part = rows // splits
    dq, dk, dv = [], [], []
    for h in (0, 1):
        i = first_head + h
        keys = cat(k, pad + one_lanes(i, 12 + i, 24 + i))
        values = cat(v, jnp.broadcast_to(one_lanes(36 + i, 48 + i, 60 + i), (rows, 128)))
        dqs, dk_sum, dv_sum = [], None, None
        for j in range(splits):
            at = slice(j * part, (j + 1) * part)
            p = jnp.exp(nt(cat(own_lanes(q[at], h), terms[at]), keys))
            dp = nt(cat(own_lanes(g[at], h), terms[at]), values)
            ds = (p * dp).astype(BF16)
            dqs.append(nn(ds, k))
            dv_part, dk_part = tn(p.astype(BF16), g[at]), tn(ds, q[at])
            dv_sum = dv_part if dv_sum is None else dv_sum + dv_part
            dk_sum = dk_part if dk_sum is None else dk_sum + dk_part
        dq.append(dqs[0] if splits == 1 else jnp.concatenate(dqs, axis=0))
        dk.append(dk_sum)
        dv.append(dv_sum)
    left = lanes() < 64
    return [jnp.where(left, t[0], t[1]).astype(BF16) for t in (dq, dk, dv)]


class Sends:
    def __init__(self, r):
        self.r = r
        self.dp, self.z = lax.axis_index("dp"), lax.axis_index("mp")
        self.y, self.x, self.c = self.dp // 4, lax.rem(self.dp // 2, 2), lax.rem(self.dp, 2)

    def device(self, y=None, x=None, c=None, z=None):
        y, x, c, z = (own if new is None else new for own, new in ((self.y, y), (self.x, x), (self.c, c), (self.z, z)))
        return (4 * y + 2 * x + c, z)

    def copy(self, src, dst, sems, index, device):
        send, recv = sems
        return pltpu.make_async_remote_copy(
            src_ref=src, dst_ref=dst, send_sem=send.at[index], recv_sem=recv.at[index],
            device_id=device, device_id_type=pl.DeviceIdType.MESH,
        )

    def partners(self):
        return [self.device(c=1 - self.c), self.device(x=1 - self.x), self.device(y=1 - self.y)] + [
            self.device(z=lax.rem(self.z + d, 4)) for d in (1, 2, 3)
        ]

    def barrier(self):
        sem = pltpu.get_barrier_semaphore()
        for device in self.partners():
            pl.semaphore_signal(sem, inc=1, device_id=device, device_id_type=pl.DeviceIdType.MESH)
        pl.semaphore_wait(sem, 6)

    def gather(self, group, cols, stage):
        r, y, x, c, z = self.r, self.y, self.x, self.c, self.z
        sems = (r.ag_send, r.ag_recv)
        if stage == 0:
            return [
                self.copy(r.wsh.at[:, cols], r.g.at[z, y, x, c, :, cols], sems, (group, d - 1), self.device(z=lax.rem(z + d, 4)))
                for d in (1, 2, 3)
            ]
        if stage == 1:
            a, b = r.g.at[:, y, x, c, 0:48, cols], r.g.at[:, y, x, c, 48:96, cols]
            return [
                self.copy(a, a, sems, (group, 3), self.device(x=1 - x)),
                self.copy(b, b, sems, (group, 4), self.device(y=1 - y)),
            ]
        if stage == 2:
            a, b = r.g.at[:, y, :, c, 0:48, cols], r.g.at[:, :, x, c, 48:96, cols]
            return [
                self.copy(a, a, sems, (group, 5), self.device(y=1 - y)),
                self.copy(b, b, sems, (group, 6), self.device(x=1 - x)),
            ]
        a = r.g.at[:, :, :, c, :, cols]
        return [self.copy(a, a, sems, (group, 7), self.device(c=1 - c))]

    def scatter(self, group, cols, stage, bufs):
        r, y, x, c, z = self.r, self.y, self.x, self.c, self.z
        sems = (r.rs_send, r.rs_recv)
        rc, r2, r1, rz = bufs
        if stage == 0:
            return [self.copy(r.g.at[:, :, :, 1 - c, :, cols], rc, sems, (group, 0), self.device(c=1 - c))]
        if stage == 1:
            return [
                self.copy(r.g.at[:, 1 - y, :, c, 0:48, cols], r2.at[0], sems, (group, 1), self.device(y=1 - y)),
                self.copy(r.g.at[:, :, 1 - x, c, 48:96, cols], r2.at[1], sems, (group, 2), self.device(x=1 - x)),
            ]
        if stage == 2:
            return [
                self.copy(r.g.at[:, y, 1 - x, c, 0:48, cols], r1.at[0], sems, (group, 3), self.device(x=1 - x)),
                self.copy(r.g.at[:, 1 - y, x, c, 48:96, cols], r1.at[1], sems, (group, 4), self.device(y=1 - y)),
            ]
        return [
            self.copy(
                r.g.at[lax.rem(z + d, 4), y, x, c, :, cols], rz.at[d - 1], sems, (group, 4 + d), self.device(z=lax.rem(z + d, 4))
            )
            for d in (1, 2, 3)
        ]

    def add_up(self, cols, stage, bufs):
        r, y, x, c, z = self.r, self.y, self.x, self.c, self.z
        rc, r2, r1, rz = bufs

        def add(index, part):
            r.g[index] = (r.g[index].astype(F32) + part.astype(F32)).astype(BF16)

        every = slice(None)
        if stage < 3:
            @pl.loop(0, 4)
            def _(m):
                if stage == 0:
                    for i in range(2):
                        add((m, i, every, c, every, cols), rc[m, i])
                elif stage == 1:
                    add((m, y, every, c, slice(0, 48), cols), r2[0, m])
                    add((m, every, x, c, slice(48, 96), cols), r2[1, m])
                else:
                    add((m, y, x, c, slice(0, 48), cols), r1[0, m])
                    add((m, y, x, c, slice(48, 96), cols), r1[1, m])
        else:
            total = r.g[z, y, x, c, :, cols].astype(F32)
            for d in range(3):
                total = total + rz[d].astype(F32)
            r.gsh[:, cols] = total


def kernel(names, comm, *refs):
    r = types.SimpleNamespace(**dict(zip(names, refs)))
    g, wb, qkv, att, h2, dy, y, e, lse, zdu, x_ref = r.g, r.wb, r.qkv, r.att, r.h2, r.dy, r.y, r.e, r.lse, r.zdu, r.x
    rank = lax.axis_index("mp")
    large = rank < 3
    small = jnp.logical_not(large)
    blocks = jnp.where(large, 1, 2)
    vrow = lambda i: r.vec[i : i + 1, :]

    def weight(z, cols):
        return g[z, :, :, :, :, cols].reshape(WIDTH, -1)

    def put_weight(z, cols, value):
        g[z, :, :, :, :, cols] = value.reshape(2, 2, 2, 96, value.shape[-1])

    group_a, group_b = slice(0, 384), slice(384, 768)

    def chunk(c):
        return pl.ds(pl.multiple_of(768 + 512 * c, 128), 512)

    if comm:
        t = Sends(r)
        groups = [(0, group_a), (1, group_b)] + [(2 + c, chunk(c)) for c in range(CHUNKS)]
        at_chunk = lambda c: (2 + c, chunk(c))

        def ag(group, stage):
            if stage > 0:
                for k in t.gather(*group, stage - 1):
                    k.wait_recv()
            if stage < 4:
                for k in t.gather(*group, stage):
                    k.start()

        def ag_sent(group):
            for stage in range(4):
                for k in t.gather(*group, stage):
                    k.wait_send()

        def bufs(group):
            index, cols = group
            width = cols.size if isinstance(cols, pl.Slice) else cols.stop - cols.start
            turn = lax.rem(index, 2) if isinstance(index, jax.Array) else index % 2
            part = slice(0, width)
            return (
                r.rc.at[turn, :, :, :, :, part], r.r2.at[turn, :, :, :, :, part],
                r.r1.at[turn, :, :, :, part], r.rz.at[turn, :, :, part],
            )

        def rs(group, stage):
            b = bufs(group)
            if stage > 0:
                for k in t.scatter(*group, stage - 1, b):
                    k.wait()
                t.add_up(group[1], stage - 1, b)
            if stage < 4:
                for k in t.scatter(*group, stage, b):
                    k.start()

        last = rank == 3
        kept = jnp.where(last, 5, 4 - rank)
        got_at = kept

        def rows_out(src, dst, i):
            for j in range(3):
                @pl.when((rank < 3) & (j <= rank))
                def _(j=j):
                    theirs = jnp.where(rank == 2, 5, 3 - rank)
                    k = t.copy(src.at[4 - rank + j], dst.at[theirs + j], (r.row_send, r.row_recv), (i, j), t.device(z=rank + 1))
                    k.start()

        def rows_out_wait(src, dst, i):
            for j in range(3):
                @pl.when((rank < 3) & (j <= rank))
                def _(j=j):
                    theirs = jnp.where(rank == 2, 5, 3 - rank)
                    t.copy(src.at[4 - rank + j], dst.at[theirs + j], (r.row_send, r.row_recv), (i, j), t.device(z=rank + 1)).wait_send()

        def rows_in_wait(src, dst, i):
            for j in range(3):
                @pl.when(j < rank)
                def _(j=j):
                    t.copy(src.at[j], dst.at[got_at + j], (r.row_send, r.row_recv), (i, j), t.device(z=rank - 1)).wait_recv()

        def own_rows(src, dst, i, start, back=False):
            for j in range(5):
                @pl.when(j < kept)
                def _(j=j):
                    a, b = (src.at[j, :, 0:WIDTH], dst.at[j, :, 0:WIDTH])
                    k = pltpu.make_async_copy(a, b, r.loc_sem.at[i, j])
                    k.start() if start else k.wait()

        def rows_back(src, dst, i):
            for j in range(3):
                @pl.when(j < rank)
                def _(j=j):
                    t.copy(src.at[got_at + j, :, 0:WIDTH], dst.at[5 - rank + j], (r.row_send, r.row_recv), (i, j), t.device(z=rank - 1)).start()

        def rows_back_wait(src, dst, i):
            for j in range(3):
                @pl.when(j < rank)
                def _(j=j):
                    t.copy(src.at[got_at + j, :, 0:WIDTH], dst.at[5 - rank + j], (r.row_send, r.row_recv), (i, j), t.device(z=rank - 1)).wait_send()

                @pl.when((rank < 3) & (j <= rank))
                def _(j=j):
                    t.copy(src.at[j, :, 0:WIDTH], dst.at[4 - rank + j], (r.row_send, r.row_recv), (i, j), t.device(z=rank + 1)).wait_recv()

        biases = [
            t.copy(r.bsh, r.bz.at[rank], (r.bias_send, r.bias_recv), d - 1, t.device(z=lax.rem(rank + d, 4))) for d in (1, 2, 3)
        ]
        t.barrier()
        own_rows(r.x_own, x_ref, 0, True)
        ag(groups[0], 0)
        for k in biases:
            k.start()
        rows_out(r.x_own, x_ref, 0)
        own_rows(r.dy_own, dy, 1, True)
        g[t.z, t.y, t.x, t.c] = r.wsh[...]
        r.bz[rank] = r.bsh[...]
    else:
        copies = [
            pltpu.make_async_copy(r.g_in, g, r.loc_sem.at[0, 0]),
            pltpu.make_async_copy(r.dy_own, dy, r.loc_sem.at[0, 1]),
            pltpu.make_async_copy(r.x_own, x_ref, r.loc_sem.at[0, 2]),
        ]
        for k in copies:
            k.start()
        for k in copies:
            k.wait()
    r.sums[...] = jnp.zeros_like(r.sums)
    r.six[...] = jnp.zeros_like(r.six)
    r.pad[...] = pad_lane(BLOCK)

    if comm:
        ag(groups[0], 1)
        ag(groups[1], 0)
        own_rows(r.x_own, x_ref, 0, False)
        rows_in_wait(r.x_own, x_ref, 0)
        ag(groups[0], 2)
        ag(groups[1], 1)
        ag(groups[2], 0)

    @pl.loop(0, blocks)
    def _(b):
        n, _s = normalize(block_of(x_ref, b).astype(F32))
        put_block(h2, b, (n * vrow(0) + vrow(1)).astype(BF16))

    if comm:
        for k in biases:
            k.wait()
        ag(groups[0], 3)
        ag(groups[1], 2)
        rows_out(r.dy_own, dy, 1)

    def bias_pair(i):
        if i < 2:
            return jnp.concatenate([r.bz[2 * i, 1:2, 0:384], r.bz[2 * i + 1, 1:2, 0:384]], axis=1)
        parts = []
        for a in (0, 2):
            for o in range(3):
                parts += [r.bz[a + m, 1:2, 384 + 64 * o : 448 + 64 * o] for m in (0, 1)]
        return jnp.concatenate(parts, axis=1)

    def w_pair(i):
        if i < 2:
            return jnp.concatenate([weight(2 * i, group_a), weight(2 * i + 1, group_a)], axis=1)
        return wb[:, 0:768]

    def project(parts):
        @pl.loop(0, blocks)
        def _(b):
            h1 = block_of(h2, b)
            for i in parts:
                out = nn(h1, w_pair(i)) + bias_pair(i)
                qkv[pl.ds(4 * b, 4), :, 768 * i : 768 * (i + 1)] = out.astype(BF16).reshape(4, ROWS, 768)

    if comm:
        ag(groups[0], 4)
        ag(groups[1], 3)
        ag(groups[2], 1)
        ag(groups[3], 0)
    project((0, 1))

    def pair_columns(ref, u0, count, p):
        return [
            ref[pl.ds(u0, count), :, pl.ds(pl.multiple_of(384 * p + 128 * i, 128), 128)].reshape(count * ROWS, 128)
            for i in range(3)
        ]

    def forward_image(u0, count, p):
        q, k, v = pair_columns(qkv, u0, count, p)
        out, logs = attend_pair(q, k, v, r.pad[0 : count * ROWS], 2 if count == 4 else 1)
        att[pl.ds(u0, count), :, pl.ds(pl.multiple_of(128 * p, 128), 128)] = out.reshape(count, ROWS, 128)
        old = lse[pl.ds(u0, count)].reshape(count * ROWS, 128)
        for h in (0, 1):
            old = jnp.where(lanes() == 2 * p + h, logs[h], old)
        lse[pl.ds(u0, count)] = old.reshape(count, ROWS, 128)

    def images(one, p):
        @pl.when(large)
        def _():
            one(0, 4, p)

        @pl.when(small)
        def _():
            @pl.loop(0, 2)
            def _(i):
                for j in range(4):
                    one(4 * i + j, 1, p)

    def ticks(p, steps):
        if comm:
            for at, functions in steps.items():
                @pl.when(p == at)
                def _(functions=functions):
                    for f in functions:
                        f()

    @pl.loop(0, 4)
    def _(p):
        images(forward_image, p)
        ticks(p, {
            0: [lambda: ag(groups[2], 2)],
            1: [lambda: ag(groups[2], 3), lambda: ag(groups[3], 1)],
            2: [lambda: ag(groups[3], 2), lambda: ag(groups[4], 0)],
            3: [lambda: ag(groups[1], 4)],
        })

    def unpack_b():
        parts = [weight(z, group_b) for z in range(4)]
        o01 = [t[:, 0:128] for t in parts]
        qs, ks, vs, o2 = ([t[:, 128 + 64 * i : 192 + 64 * i] for t in parts] for i in range(4))
        cols = []
        for i in (0, 2):
            cols += [cat(qs[i], qs[i + 1]), cat(ks[i], ks[i + 1]), cat(vs[i], vs[i + 1])]
        cols += o01 + [cat(o2[0], o2[1]), cat(o2[2], o2[3])]
        for i, part in enumerate(cols):
            wb[:, 128 * i : 128 * (i + 1)] = part

    unpack_b()
    project((2,))

    @pl.loop(4, 6)
    def _(p):
        images(forward_image, p)
        ticks(p, {
            4: [lambda: ag(groups[3], 3), lambda: ag(groups[4], 1)],
            5: [lambda: ag(groups[2], 4), lambda: ag(groups[4], 2)],
        })

    def middle_of(b):
        return block_of(x_ref, b).astype(F32) + nt(block_of(att, b), wb[:, 768:1536]) + vrow(4)

    @pl.loop(0, blocks)
    def _(b):
        mid = middle_of(b)
        n, _s = normalize(mid)
        put_block(h2, b, (n * vrow(2) + vrow(3)).astype(BF16))
        put_block(y, b, mid + vrow(5))
        put_block(e, b, jnp.zeros((BLOCK, WIDTH), F32))

    if comm:
        own_rows(r.dy_own, dy, 1, False)
        rows_in_wait(r.dy_own, dy, 1)
        ag_sent(groups[2])

    @pl.loop(0, CHUNKS)
    def _(c):
        @pl.loop(0, 2)
        def _(zp):
            at = pl.multiple_of(768 + 512 * c, 128)
            ucols, dcols = pl.ds(at, 256), pl.ds(pl.multiple_of(at + 256, 128), 256)
            up = jnp.concatenate([weight(2 * zp, ucols), weight(2 * zp + 1, ucols)], axis=1)
            down = jnp.concatenate([weight(2 * zp, dcols), weight(2 * zp + 1, dcols)], axis=1)
            bcols = pl.ds(pl.multiple_of(256 * c, 128), 256)
            hb = jnp.concatenate([r.bz[2 * zp, 0:1, bcols], r.bz[2 * zp + 1, 0:1, bcols]], axis=1)

            @pl.loop(0, blocks)
            def _(b):
                u = nn(block_of(h2, b), up) + hb
                dz = nn(block_of(dy, b), down)
                big_phi, small_phi = gelu_terms(u)
                z = (u * big_phi).astype(BF16)
                du = (dz * (big_phi + small_phi)).astype(BF16)
                zdu[pl.ds(4 * b, 4), :, 0:512] = z.reshape(4, ROWS, 512)
                zdu[pl.ds(4 * b, 4), :, 512:1024] = du.reshape(4, ROWS, 512)
                r.six[2 * c + zp, 0:1, :] += column_sums(du.astype(F32))
                put_block(y, b, block_of(y, b) + nt(z, down))
                put_block(e, b, block_of(e, b) + nt(du, up))

            def grads(count):
                rows = count * ROWS
                h2v, dyv = h2[0:count].reshape(rows, WIDTH), dy[0:count].reshape(rows, WIDTH)
                gu = tn(h2v, zdu[0:count, :, 512:1024].reshape(rows, 512)).astype(BF16)
                gd = tn(dyv, zdu[0:count, :, 0:512].reshape(rows, 512)).astype(BF16)
                for i in range(2):
                    put_weight(2 * zp + i, ucols, gu[:, 256 * i : 256 * (i + 1)])
                    put_weight(2 * zp + i, dcols, gd[:, 256 * i : 256 * (i + 1)])

            pl.when(large)(lambda: grads(4))
            pl.when(small)(lambda: grads(8))

            if comm:
                @pl.when((zp == 0) & (c == 0))
                def _():
                    ag(groups[3], 4)
                    ag_sent(groups[3])
                    ag(groups[4], 3)

                @pl.when((zp == 1) & (c == 0))
                def _():
                    ag(groups[4], 4)
                    ag_sent(groups[4])

                @pl.when((zp == 0) & (c > 0))
                def _():
                    rs(at_chunk(c - 1), 1)

                @pl.when((zp == 0) & (c == 2))
                def _():
                    rs(at_chunk(0), 3)

                @pl.when((zp == 1) & (c > 0))
                def _():
                    rs(at_chunk(c - 1), 2)

                @pl.when((zp == 1) & (c == 2))
                def _():
                    rs(at_chunk(0), 4)

                @pl.when(zp == 1)
                def _():
                    rs(at_chunk(c), 0)

    @pl.loop(0, blocks)
    def _(b):
        zdu[pl.ds(4 * b, 4), :, 0:768] = block_of(y, b).astype(BF16).reshape(4, ROWS, WIDTH)
        n, scale = normalize(middle_of(b))
        grad = block_of(e, b)
        dyv = block_of(dy, b).astype(F32)
        dmid = dyv + norm_back(grad, vrow(2), n, scale)
        r.sums[2:3, :] += column_sums(grad * n)
        r.sums[3:4, :] += column_sums(grad)
        r.sums[4:5, :] += column_sums(dmid)
        r.sums[5:6, :] += column_sums(dyv)
        put_block(e, b, dmid)
        put_block(h2, b, dmid.astype(BF16))

    if comm:
        own_rows(zdu, r.yout, 2, True)
        rows_back(zdu, r.yout, 2)
        rs(at_chunk(1), 3)
        rs(at_chunk(2), 1)
        ag_sent(groups[0])
        ag_sent(groups[1])
    else:
        out_copy = pltpu.make_async_copy(zdu.at[:, :, 0:768], r.yout, r.loc_sem.at[0, 0])
        out_copy.start()

    def out_grads(count):
        rows = count * ROWS
        go = tn(h2[0:count].reshape(rows, WIDTH), att[0:count].reshape(rows, WIDTH)).astype(BF16)
        for z in range(4):
            put_weight(z, slice(384, 512), go[:, 128 * z : 128 * (z + 1)])
            put_weight(z, slice(704, 768), go[:, 512 + 64 * z : 576 + 64 * z])

    pl.when(large)(lambda: out_grads(4))
    pl.when(small)(lambda: out_grads(8))

    @pl.loop(0, blocks)
    def _(b):
        d_att = nn(block_of(h2, b), wb[:, 768:1536]).astype(BF16)
        put_block(dy, b, d_att)
        prod = d_att.astype(F32) * block_of(att, b).astype(F32)
        high = prod.astype(BF16)
        feature, lane = (lax.broadcasted_iota(jnp.int32, (WIDTH, 128), i) for i in (0, 1))
        heads = jnp.where(feature // HEAD_DIM == lane, 1.0, 0.0).astype(BF16)
        dots = nn(high, heads) + nn((prod - high.astype(F32)).astype(BF16), heads)
        logs = jnp.where(lanes() < 12, block_of(lse, b), 0.0)
        terms = jnp.where(lanes() == 127, -1.0, 0.0)
        for i, part in enumerate(split_three(logs) + split_three(dots)):
            terms = terms + (part if i == 0 else pltpu.roll(part, 12 * i, axis=1))
        put_block(r.terms, b, (-terms).astype(BF16))

    def backward_image(u0, count, p):
        rows = count * ROWS
        q, k, v = pair_columns(qkv, u0, count, p)
        at = pl.multiple_of(128 * p, 128)
        grad = dy[pl.ds(u0, count), :, pl.ds(at, 128)].reshape(rows, 128)
        terms = r.terms[pl.ds(u0, count)].reshape(rows, 128)
        parts = attend_pair_back(q, k, v, grad, terms, 2 * p, r.pad[0:rows], 2 if count == 4 else 1)
        for i, part in enumerate(parts):
            qkv[pl.ds(u0, count), :, pl.ds(pl.multiple_of(384 * p + 128 * i, 128), 128)] = part.reshape(count, ROWS, 128)
        r.six[p, 1:2, 0:128] += column_sums(parts[0].astype(F32))
        r.six[p, 1:2, 128:256] += column_sums(parts[2].astype(F32))

    @pl.loop(4, 6)
    def _(p):
        images(backward_image, p)
        ticks(p, {
            4: [lambda: rs(at_chunk(1), 4), lambda: rs(at_chunk(2), 2)],
            5: [lambda: rs(at_chunk(2), 3)],
        })

    @pl.loop(0, blocks)
    def _(b):
        n, _s = normalize(block_of(x_ref, b).astype(F32))
        put_block(h2, b, (n * vrow(0) + vrow(1)).astype(BF16))

    def in_grads(count, i):
        rows = count * ROWS
        h1 = h2[0:count].reshape(rows, WIDTH)
        gq = tn(h1, qkv[0:count, :, 768 * i : 768 * (i + 1)].reshape(rows, 768)).astype(BF16)
        if i < 2:
            put_weight(2 * i, group_a, gq[:, 0:384])
            put_weight(2 * i + 1, group_a, gq[:, 384:768])
        else:
            for z in range(4):
                base = 384 * (z // 2) + 64 * (z % 2)
                for o in range(3):
                    put_weight(z, slice(512 + 64 * o, 576 + 64 * o), gq[:, base + 128 * o : base + 128 * o + 64])

    pl.when(large)(lambda: in_grads(4, 2))
    pl.when(small)(lambda: in_grads(8, 2))
    if comm:
        rs(groups[1], 0)

    @pl.loop(0, 4)
    def _(p):
        images(backward_image, p)
        ticks(p, {
            0: [lambda: rs(at_chunk(2), 4), lambda: rs(groups[1], 1)],
            1: [lambda: rs(groups[1], 2)],
            2: [lambda: rs(groups[1], 3)],
            3: [lambda: rs(groups[1], 4)],
        })

    @pl.loop(0, blocks)
    def _(b):
        grad = nt(block_of(qkv, b)[:, 0:768], w_pair(0))
        grad += nt(block_of(qkv, b)[:, 768:1536], w_pair(1))
        grad += nt(block_of(qkv, b)[:, 1536:2304], w_pair(2))
        put_block(y, b, grad)

    for i in range(2):
        pl.when(large)(lambda i=i: in_grads(4, i))
        pl.when(small)(lambda i=i: in_grads(8, i))
    if comm:
        rs(groups[0], 0)
        own_rows(zdu, r.yout, 2, False)
        rows_back_wait(zdu, r.yout, 2)
    else:
        out_copy.wait()

    @pl.loop(0, blocks)
    def _(b):
        n, scale = normalize(block_of(x_ref, b).astype(F32))
        grad = block_of(y, b)
        r.sums[0:1, :] += column_sums(grad * n)
        r.sums[1:2, :] += column_sums(grad)
        out = block_of(e, b) + norm_back(grad, vrow(0), n, scale)
        zdu[pl.ds(4 * b, 4), :, 0:768] = out.astype(BF16).reshape(4, ROWS, WIDTH)

    for s in range(6):
        for i in range(2):
            hidden = 512 * s + 256 * i
            r.sums[6 + hidden // 768 : 7 + hidden // 768, hidden % 768 : hidden % 768 + 256] = r.six[s, 0:1, 256 * i : 256 * (i + 1)]
            r.sums[10 + i : 11 + i, 128 * s : 128 * (s + 1)] = r.six[s, 1:2, 128 * i : 128 * (i + 1)]

    if not comm:
        last_copies = [
            pltpu.make_async_copy(zdu.at[:, :, 0:768], r.gin, r.loc_sem.at[0, 0]),
            pltpu.make_async_copy(g, r.gout, r.loc_sem.at[0, 1]),
        ]
        for k in last_copies:
            k.start()
        for k in last_copies:
            k.wait()
        return

    own_rows(zdu, r.gin, 3, True)
    rows_back(zdu, r.gin, 3)

    def sum_step(slot, device):
        k = t.copy(r.sums, r.sum_in.at[slot], (r.sum_send, r.sum_recv), slot, device)
        k.start()
        return k

    for stage in range(3):
        k = sum_step(stage, t.partners()[stage])
        rs(groups[0], stage + 1)
        k.wait()
        r.sums[...] += r.sum_in[stage]
    steps = [sum_step(2 + d, t.device(z=lax.rem(rank + d, 4))) for d in (1, 2, 3)]
    rs(groups[0], 4)
    for k in steps:
        k.wait()
    r.total[...] = r.sums[...] + r.sum_in[3] + r.sum_in[4] + r.sum_in[5]
    own_rows(zdu, r.gin, 3, False)
    rows_back_wait(zdu, r.gin, 3)
    rows_out_wait(r.x_own, x_ref, 0)
    rows_out_wait(r.dy_own, dy, 1)


def run_kernel(comm, x, dy, weights, vectors, biases):
    vmem, hbm = pl.BlockSpec(memory_space=pltpu.VMEM), pl.BlockSpec(memory_space=pl.ANY)
    units, own = (UNITS, ROWS, WIDTH), (x.shape[0], ROWS, WIDTH)
    shape = jax.ShapeDtypeStruct
    sem = pltpu.SemaphoreType.DMA
    ins = ["x_own", "dy_own", "wsh" if comm else "g_in", "vec", "bsh" if comm else "bz"]
    in_specs = [hbm, hbm, vmem if comm else hbm, vmem, vmem]
    outs = {"yout": (shape(own, BF16), hbm), "gin": (shape(own, BF16), hbm)}
    if comm:
        outs |= {"gsh": (shape((96, COLS), F32), vmem), "total": (shape((16, WIDTH), F32), vmem)}
    else:
        outs |= {"gout": (shape((4, 2, 2, 2, 96, COLS), BF16), hbm), "sums": (shape((16, WIDTH), F32), vmem)}
    scratch = {
        "g": pltpu.VMEM((4, 2, 2, 2, 96, COLS), BF16),
        "wb": pltpu.VMEM((WIDTH, 1536), BF16),
        "x": pltpu.VMEM(units, BF16),
        "qkv": pltpu.VMEM((UNITS, ROWS, COLS), BF16),
        "att": pltpu.VMEM(units, BF16),
        "h2": pltpu.VMEM(units, BF16),
        "dy": pltpu.VMEM(units, BF16),
        "y": pltpu.VMEM(units, F32),
        "e": pltpu.VMEM(units, F32),
        "lse": pltpu.VMEM((UNITS, ROWS, 128), F32),
        "zdu": pltpu.VMEM((UNITS, ROWS, 1024), BF16),
        "terms": pltpu.VMEM((UNITS, ROWS, 128), BF16),
        "pad": pltpu.VMEM((BLOCK, 128), BF16),
        "six": pltpu.VMEM((6, 8, 512), F32),
        "loc_sem": sem((4, 5)),
    }
    if comm:
        scratch |= {
            "sums": pltpu.VMEM((16, WIDTH), F32),
            "sum_in": pltpu.VMEM((6, 16, WIDTH), F32),
            "bz": pltpu.VMEM((4, 8, WIDTH), F32),
            "rc": pltpu.VMEM((2, 4, 2, 2, 96, 512), BF16),
            "r2": pltpu.VMEM((2, 2, 4, 2, 48, 512), BF16),
            "r1": pltpu.VMEM((2, 2, 4, 48, 512), BF16),
            "rz": pltpu.VMEM((2, 3, 96, 512), BF16),
            "ag_send": sem((5, 8)), "ag_recv": sem((5, 8)),
            "rs_send": sem((5, 8)), "rs_recv": sem((5, 8)),
            "row_send": sem((4, 3)), "row_recv": sem((4, 3)),
            "bias_send": sem((3,)), "bias_recv": sem((3,)),
            "sum_send": sem((6,)), "sum_recv": sem((6,)),
        }
    params = dict(collective_id=0, has_side_effects=True) if comm else {}
    return pl.pallas_call(
        functools.partial(kernel, ins + list(outs) + list(scratch), comm),
        out_shape=[v[0] for v in outs.values()],
        in_specs=in_specs,
        out_specs=[v[1] for v in outs.values()],
        scratch_shapes=list(scratch.values()),
        compiler_params=pltpu.CompilerParams(vmem_limit_bytes=64 * 2**20 - 2**16, **params),
    )(x, dy, weights, vectors, biases)


def pack_shard(attention_in, attention_out, hidden_in, hidden_out):
    q, k, v = attention_in[:, 0] * 0.125, attention_in[:, 1], attention_in[:, 2]
    out_t, down_t = attention_out.T, hidden_out.T
    cols = [q[:, :128], k[:, :128], v[:, :128], out_t[:, :128], q[:, 128:], k[:, 128:], v[:, 128:], out_t[:, 128:]]
    for c in range(CHUNKS):
        cols += [hidden_in[:, 256 * c : 256 * (c + 1)], down_t[:, 256 * c : 256 * (c + 1)]]
    return jnp.concatenate([t.astype(BF16) for t in cols], axis=1)


def unpack_shard(grad):
    q = jnp.concatenate([grad[:, 0:128], grad[:, 512:576]], axis=1) * 0.125
    k = jnp.concatenate([grad[:, 128:256], grad[:, 576:640]], axis=1)
    v = jnp.concatenate([grad[:, 256:384], grad[:, 640:704]], axis=1)
    out_t = jnp.concatenate([grad[:, 384:512], grad[:, 704:768]], axis=1)
    up = jnp.concatenate([grad[:, 768 + 512 * c : 1024 + 512 * c] for c in range(CHUNKS)], axis=1)
    down = jnp.concatenate([grad[:, 1024 + 512 * c : 1280 + 512 * c] for c in range(CHUNKS)], axis=1)
    return jnp.stack([q, k, v], axis=1), out_t.T, up, down.T


def nesterov(weight_old, moment_old, average_old, gradient, rate, decay):
    step_dir = gradient + decay * weight_old
    moment_new = MOMENTUM * moment_old + step_dir
    weight_new = weight_old - rate * (step_dir + MOMENTUM * moment_new)
    return (weight_new, moment_new, AVERAGE * average_old + (1.0 - AVERAGE) * weight_new)


def local(
    tokens, cotangent, slot_live,
    vectors, vectors_momentum, vectors_average,
    column_bias, column_bias_momentum, column_bias_average,
    hidden_bias, hidden_bias_momentum, hidden_bias_average,
    attention_in, attention_in_momentum, attention_in_average,
    attention_out, attention_out_momentum, attention_out_average,
    hidden_in, hidden_in_momentum, hidden_in_average,
    hidden_out, hidden_out_momentum, hidden_out_average,
):
    rows_dev = tokens.shape[0]
    rank = lax.axis_index("mp")
    total_rows = rows_dev * lax.axis_size("mp") * lax.axis_size("dp")
    own_units = rows_dev // UNIT
    unit = rank * own_units + jnp.arange(own_units, dtype=jnp.int32)
    slot = jnp.where(unit < 4 * SLOT_L, unit // 4, unit - 3 * SLOT_L)
    live = jnp.sum(
        jnp.where(slot[:, None] == jnp.arange(slot_live.shape[1], dtype=jnp.int32)[None], slot_live, 0), axis=1
    ).astype(BF16)

    def in_units(rows):
        return jnp.pad(rows.reshape(own_units, UNIT, WIDTH), ((0, 0), (0, ROWS - UNIT), (0, 0)))

    def to_work(units):
        got = lax.ppermute(units[2:5], "mp", [(0, 1), (1, 2), (2, 3)])
        kept = jnp.where(rank == 3, 5, 4 - rank)
        index = jnp.arange(UNITS, dtype=jnp.int32)
        pick = jnp.where(index < kept, index, jnp.clip(8 - rank + index - kept, 5, 7))
        return jnp.take(jnp.concatenate([units, got], axis=0), pick, axis=0)

    def from_work(work):
        kept = jnp.where(rank == 3, 5, 4 - rank)
        theirs = lax.dynamic_slice_in_dim(work, kept, 3, 0)
        got = lax.ppermute(theirs, "mp", [(1, 0), (2, 1), (3, 2)])
        index = jnp.arange(own_units, dtype=jnp.int32)
        row = jnp.concatenate([work, got], axis=0)
        pick = jnp.where(index < kept, index, 8 + index - kept)
        units = jnp.take(row, pick, axis=0)
        return units[:, :UNIT].reshape(rows_dev, WIDTH)

    x, dy = in_units(tokens), in_units(cotangent) * live[:, None, None]
    shard = pack_shard(attention_in, attention_out, hidden_in, hidden_out)
    bq, bv = column_bias[0] * 0.125, column_bias[1]
    none = jnp.zeros((128,), F32)
    row = jnp.concatenate([bq[:128], none, bv[:128], bq[128:], none[:64], bv[128:], none, none[:64]])
    bias_rows = jnp.concatenate([hidden_bias[None], row[None], jnp.zeros((6, WIDTH), F32)], axis=0)

    if lax.axis_size("dp") == 8:
        yout, gin, reduced, total = run_kernel(True, x, dy, shard, vectors, bias_rows)
        block_output, input_gradient = (t[:, :UNIT].reshape(rows_dev, WIDTH) for t in (yout, gin))
    else:
        weights = lax.all_gather(lax.all_gather(shard, "dp", axis=0, tiled=True), "mp", axis=0)
        weights = weights.reshape(4, 2, 2, 2, 96, COLS)
        all_bias = lax.all_gather(bias_rows, "mp", axis=0)
        yout, gin, grads, total = run_kernel(False, to_work(x), to_work(dy), weights, vectors, all_bias)
        block_output, input_gradient = from_work(yout), from_work(gin)
        reduced = lax.psum_scatter(grads.reshape(4, WIDTH, COLS), "mp", scatter_dimension=0, tiled=True)[0]
        reduced = lax.psum_scatter(reduced, "dp", scatter_dimension=0, tiled=True).astype(F32)
        total = lax.psum(total, ("dp", "mp"))
    vector_grad = total[0:6]
    hidden_grad = jnp.transpose(total[6:10].reshape(CHUNKS, 2, 2, 256), (1, 2, 0, 3)).reshape(4, 768)
    hidden_grad = lax.dynamic_index_in_dim(hidden_grad, rank, 0, keepdims=False)
    pq, pv = total[10].reshape(PAIRS, 2, 64), total[11].reshape(PAIRS, 2, 64)

    def own_heads(pairs):
        second = pairs[4:6].reshape(4, 64)
        return jnp.concatenate(
            [lax.dynamic_index_in_dim(pairs, rank, 0, keepdims=False).reshape(128),
             lax.dynamic_index_in_dim(second, rank, 0, keepdims=False)]
        )

    column_grad = jnp.stack([own_heads(pq) * 0.125, own_heads(pv)])
    gqkv, gout, gup, gdown = unpack_shard(reduced)
    root = math.sqrt(total_rows)
    steps = (
        (vectors, vectors_momentum, vectors_average, vector_grad, RATE_VECTORS, 0.0),
        (column_bias, column_bias_momentum, column_bias_average, column_grad, RATE_COLUMN, 0.0),
        (hidden_bias, hidden_bias_momentum, hidden_bias_average, hidden_grad, RATE_HIDDEN, 0.0),
        (attention_in, attention_in_momentum, attention_in_average, gqkv, RATE_ATTENTION_IN, DECAY),
        (attention_out, attention_out_momentum, attention_out_average, gout, RATE_ATTENTION_OUT, DECAY),
        (hidden_in, hidden_in_momentum, hidden_in_average, gup, RATE_HIDDEN_IN, DECAY),
        (hidden_out, hidden_out_momentum, hidden_out_average, gdown, RATE_HIDDEN_OUT, DECAY),
    )
    outs = [block_output, input_gradient]
    for weight, moment, average, gradient, rate, decay in steps:
        outs.extend(nesterov(weight, moment, average, gradient, rate / root, decay))
    return tuple(outs)


def solution(mesh):
    rows, matrix, side = P(("dp", "mp"), None), P("dp", None, "mp"), P("mp", "dp")
    params = [P()] * 3 + [P(None, "mp")] * 3 + [P("mp")] * 3 + [matrix] * 3 + [side] * 3 + [P("dp", "mp")] * 3 + [side] * 3
    return jax.shard_map(
        local,
        mesh=mesh,
        in_specs=(rows, rows, P("dp", None), *params),
        out_specs=(rows, rows, *params),
        check_vma=False,
    )
```

```python
import functools
import math
import types

import jax
import jax.numpy as jnp
from jax import lax
from jax.experimental import pallas as pl
from jax.experimental.pallas import tpu as pltpu
from jax.sharding import PartitionSpec as P

F32, BF16 = jnp.float32, jnp.bfloat16
WIDTH = 768
HEAD_DIM = 64
PATCH_L = 784
PATCH_S = 196
SLOT_L = 3
SLOT_S = 8
UNIT = 196
ROWS = 208
UNITS = 7
PAIRS = 6
CHUNKS = 3
COLS = 2304

EPSILON = 1e-06
MOMENTUM = 0.9
AVERAGE = 0.8
DECAY = 0.0001
RATE_VECTORS = 0.06
RATE_COLUMN = 0.01
RATE_HIDDEN = 0.4
RATE_ATTENTION_IN = 0.005
RATE_ATTENTION_OUT = 0.5
RATE_HIDDEN_IN = 0.05
RATE_HIDDEN_OUT = 0.015


def nn(a, b):
    return lax.dot_general(a, b, (((1,), (0,)), ((), ())), preferred_element_type=F32)


def nt(a, b):
    return lax.dot_general(a, b, (((1,), (1,)), ((), ())), preferred_element_type=F32)


def tn(a, b):
    return lax.dot_general(a, b, (((0,), (0,)), ((), ())), preferred_element_type=F32)


def normalize(values):
    centred = values - jnp.mean(values, axis=-1, keepdims=True)
    spread = jnp.mean(centred * centred, axis=-1, keepdims=True)
    scale = lax.rsqrt(spread + EPSILON)
    return centred * scale, scale


def norm_back(cotangent, gain, n, scale):
    cg = cotangent * gain
    return scale * (
        cg - jnp.mean(cg, axis=-1, keepdims=True) - n * jnp.mean(cg * n, axis=-1, keepdims=True)
    )


def column_sums(values):
    return jnp.sum(values, axis=0, keepdims=True)


def split_three(values):
    high = values.astype(BF16).astype(F32)
    mid = (values - high).astype(BF16).astype(F32)
    return high, mid, values - high - mid


def gelu_terms(u):
    e = jnp.exp(u * u * -0.5)
    k = 1.0 / (1.0 + jnp.abs(u) * (0.3275911 * math.sqrt(0.5)))
    poly = k * (
        0.5 * 0.254829592
        + k * (0.5 * -0.284496736 + k * (0.5 * 1.421413741 + k * (0.5 * -1.453152027 + k * (0.5 * 1.061405429))))
    )
    tail = poly * e
    big_phi = jnp.where(u < 0.0, tail, 1.0 - tail)
    return big_phi, u * e * (1.0 / math.sqrt(2.0 * math.pi))


def rows_of(ref, u0, count):
    return ref[u0 : u0 + count].reshape(count * ROWS, ref.shape[-1])


def put_rows(ref, u0, count, value):
    ref[u0 : u0 + count] = value.reshape(count, ROWS, value.shape[-1])


def lanes():
    return lax.broadcasted_iota(jnp.int32, (1, 128), 1)


def pad_lane(rows):
    at = lax.broadcasted_iota(jnp.int32, (rows, 128), 0)
    lane = lax.broadcasted_iota(jnp.int32, (rows, 128), 1)
    return jnp.where((lax.rem(at, ROWS) >= UNIT) & (lane == 127), -1e30, 0.0).astype(BF16)


def own_lanes(values, h):
    mask = jnp.where((lanes() < 64) == (h == 0), 1.0, 0.0).astype(BF16)
    return values * mask


def cat(*parts):
    return jnp.concatenate(parts, axis=1)


def one_lanes(*which):
    hit = functools.reduce(jnp.logical_or, [lanes() == w for w in which])
    return jnp.where(hit, 1.0, 0.0).astype(BF16)


def attend_pair(q, k, v, pad):
    keys = cat(k, pad)
    ones = jnp.broadcast_to(one_lanes(127), (q.shape[0], 128))
    outs, logs = [], []
    for h in (0, 1):
        s = nt(cat(own_lanes(q, h), ones), keys)
        top = jnp.max(s, axis=-1, keepdims=True)
        e = jnp.exp(s - top)
        total = jnp.sum(e, axis=-1, keepdims=True)
        outs.append(nn(e.astype(BF16), v) * (1.0 / total))
        logs.append(top + jnp.log(total))
    return jnp.where(lanes() < 64, outs[0], outs[1]).astype(BF16), logs


def attend_pair_back(q, k, v, g, terms, first_head, pad):
    dq, dk, dv = [], [], []
    for h in (0, 1):
        i = first_head + h
        keys = cat(k, pad + one_lanes(i, 12 + i, 24 + i))
        values = cat(v, jnp.broadcast_to(one_lanes(36 + i, 48 + i, 60 + i), v.shape))
        p = jnp.exp(nt(cat(own_lanes(q, h), terms), keys))
        dp = nt(cat(own_lanes(g, h), terms), values)
        ds = (p * dp).astype(BF16)
        dv.append(tn(p.astype(BF16), g))
        dq.append(nn(ds, k))
        dk.append(tn(ds, q))
    left = lanes() < 64
    return [jnp.where(left, t[0], t[1]).astype(BF16) for t in (dq, dk, dv)]


class Sends:
    def __init__(self, r):
        self.r = r
        self.dp, self.z = lax.axis_index("dp"), lax.axis_index("mp")
        self.y, self.x, self.c = self.dp // 4, lax.rem(self.dp // 2, 2), lax.rem(self.dp, 2)

    def device(self, y=None, x=None, c=None, z=None):
        y, x, c, z = (own if new is None else new for own, new in ((self.y, y), (self.x, x), (self.c, c), (self.z, z)))
        return (4 * y + 2 * x + c, z)

    def copy(self, src, dst, sems, index, device):
        send, recv = sems
        return pltpu.make_async_remote_copy(
            src_ref=src, dst_ref=dst, send_sem=send.at[index], recv_sem=recv.at[index],
            device_id=device, device_id_type=pl.DeviceIdType.MESH,
        )

    def partners(self):
        return [self.device(c=1 - self.c), self.device(x=1 - self.x), self.device(y=1 - self.y)] + [
            self.device(z=lax.rem(self.z + d, 4)) for d in (1, 2, 3)
        ]

    def barrier(self):
        sem = pltpu.get_barrier_semaphore()
        for device in self.partners():
            pl.semaphore_signal(sem, inc=1, device_id=device, device_id_type=pl.DeviceIdType.MESH)
        pl.semaphore_wait(sem, 6)

    def gather(self, group, cols, stage):
        r, y, x, c, z = self.r, self.y, self.x, self.c, self.z
        sems = (r.ag_send, r.ag_recv)
        if stage == 0:
            return [
                self.copy(r.wsh.at[:, cols], r.g.at[z, y, x, c, :, cols], sems, (group, d - 1), self.device(z=lax.rem(z + d, 4)))
                for d in (1, 2, 3)
            ]
        if stage == 1:
            a, b = r.g.at[:, y, x, c, 0:48, cols], r.g.at[:, y, x, c, 48:96, cols]
            return [
                self.copy(a, a, sems, (group, 3), self.device(x=1 - x)),
                self.copy(b, b, sems, (group, 4), self.device(y=1 - y)),
            ]
        if stage == 2:
            a, b = r.g.at[:, y, :, c, 0:48, cols], r.g.at[:, :, x, c, 48:96, cols]
            return [
                self.copy(a, a, sems, (group, 5), self.device(y=1 - y)),
                self.copy(b, b, sems, (group, 6), self.device(x=1 - x)),
            ]
        a = r.g.at[:, :, :, c, :, cols]
        return [self.copy(a, a, sems, (group, 7), self.device(c=1 - c))]

    def scatter(self, group, cols, stage, bufs):
        r, y, x, c, z = self.r, self.y, self.x, self.c, self.z
        sems = (r.rs_send, r.rs_recv)
        rc, r2, r1, rz = bufs
        if stage == 0:
            return [self.copy(r.g.at[:, :, :, 1 - c, :, cols], rc, sems, (group, 0), self.device(c=1 - c))]
        if stage == 1:
            return [
                self.copy(r.g.at[:, 1 - y, :, c, 0:48, cols], r2.at[0], sems, (group, 1), self.device(y=1 - y)),
                self.copy(r.g.at[:, :, 1 - x, c, 48:96, cols], r2.at[1], sems, (group, 2), self.device(x=1 - x)),
            ]
        if stage == 2:
            return [
                self.copy(r.g.at[:, y, 1 - x, c, 0:48, cols], r1.at[0], sems, (group, 3), self.device(x=1 - x)),
                self.copy(r.g.at[:, 1 - y, x, c, 48:96, cols], r1.at[1], sems, (group, 4), self.device(y=1 - y)),
            ]
        return [
            self.copy(
                r.g.at[lax.rem(z + d, 4), y, x, c, :, cols], rz.at[d - 1], sems, (group, 4 + d), self.device(z=lax.rem(z + d, 4))
            )
            for d in (1, 2, 3)
        ]

    def add_up(self, cols, stage, bufs):
        r, y, x, c, z = self.r, self.y, self.x, self.c, self.z
        rc, r2, r1, rz = bufs

        def add(index, part):
            r.g[index] = (r.g[index].astype(F32) + part.astype(F32)).astype(BF16)

        every = slice(None)
        if stage < 3:
            @pl.loop(0, 4)
            def _(m):
                if stage == 0:
                    for i in range(2):
                        add((m, i, every, c, every, cols), rc[m, i])
                elif stage == 1:
                    add((m, y, every, c, slice(0, 48), cols), r2[0, m])
                    add((m, every, x, c, slice(48, 96), cols), r2[1, m])
                else:
                    add((m, y, x, c, slice(0, 48), cols), r1[0, m])
                    add((m, y, x, c, slice(48, 96), cols), r1[1, m])
        else:
            total = r.g[z, y, x, c, :, cols].astype(F32)
            for d in range(3):
                total = total + rz[d].astype(F32)
            r.gsh[:, cols] = total


def kernel(names, comm, *refs):
    r = types.SimpleNamespace(**dict(zip(names, refs)))
    g, wb, qkv, att, h2, dy, y, e, lse, zdu, x_ref = r.g, r.wb, r.qkv, r.att, r.h2, r.dy, r.y, r.e, r.lse, r.zdu, r.x
    rank = lax.axis_index("mp")

    def blocks(f):
        pl.when(rank != 2)(lambda: f(0, 4))
        pl.when(rank == 2)(lambda: f(0, 5))
        pl.when(rank == 3)(lambda: f(4, 3))

    def whole(f):
        pl.when(rank < 2)(lambda: f(4))
        pl.when(rank == 2)(lambda: f(5))
        pl.when(rank == 3)(lambda: f(7))

    vrow = lambda i: r.vec[i : i + 1, :]

    def weight(z, cols):
        return g[z, :, :, :, :, cols].reshape(WIDTH, -1)

    def put_weight(z, cols, value):
        g[z, :, :, :, :, cols] = value.reshape(2, 2, 2, 96, value.shape[-1])

    group_a, group_b = slice(0, 384), slice(384, 768)

    def chunk(c):
        return pl.ds(pl.multiple_of(768 + 512 * c, 128), 512)

    if comm:
        t = Sends(r)
        groups = [(0, group_a), (1, group_b)] + [(2 + c, chunk(c)) for c in range(CHUNKS)]
        at_chunk = lambda c: (2 + c, chunk(c))

        def ag(group, stage):
            if stage > 0:
                for k in t.gather(*group, stage - 1):
                    k.wait_recv()
            if stage < 4:
                for k in t.gather(*group, stage):
                    k.start()

        def ag_sent(group):
            for stage in range(4):
                for k in t.gather(*group, stage):
                    k.wait_send()

        def bufs(group):
            index, cols = group
            width = cols.size if isinstance(cols, pl.Slice) else cols.stop - cols.start
            turn = lax.rem(index, 2) if isinstance(index, jax.Array) else index % 2
            part = slice(0, width)
            return (
                r.rc.at[turn, :, :, :, :, part], r.r2.at[turn, :, :, :, :, part],
                r.r1.at[turn, :, :, :, part], r.rz.at[turn, :, :, part],
            )

        def rs(group, stage):
            b = bufs(group)
            if stage > 0:
                for k in t.scatter(*group, stage - 1, b):
                    k.wait()
                t.add_up(group[1], stage - 1, b)
            if stage < 4:
                for k in t.scatter(*group, stage, b):
                    k.start()

        sent = jnp.where(rank == 0, 1, jnp.where(rank == 3, 0, 2))
        got = jnp.where(rank == 0, 0, jnp.where(rank == 1, 1, 2))
        got_at = jnp.where(rank == 1, 3, jnp.where(rank == 2, 2, 5))
        theirs_at = jnp.where(rank == 0, 3, jnp.where(rank == 1, 2, 5))
        row_sems = (r.row_send, r.row_recv)

        def place(j):
            return jnp.where((rank == 2) & (j == 2), 4, j)

        def rows_out(src, dst, i, wait=False):
            for j in range(2):
                @pl.when(j < sent)
                def _(j=j):
                    k = t.copy(src.at[5 - sent + j], dst.at[theirs_at + j], row_sems, (i, j), t.device(z=rank + 1))
                    k.wait_send() if wait else k.start()

        def rows_in_wait(src, dst, i):
            for j in range(2):
                @pl.when(j < got)
                def _(j=j):
                    t.copy(src.at[j], dst.at[got_at + j], row_sems, (i, j), t.device(z=rank - 1)).wait_recv()

        def rows_back(src, dst, i):
            for j in range(2):
                @pl.when(j < got)
                def _(j=j):
                    t.copy(src.at[got_at + j, :, 0:WIDTH], dst.at[5 - got + j], row_sems, (i, j), t.device(z=rank - 1)).start()

        def rows_back_wait(src, dst, i):
            for j in range(2):
                @pl.when(j < got)
                def _(j=j):
                    t.copy(src.at[got_at + j, :, 0:WIDTH], dst.at[5 - got + j], row_sems, (i, j), t.device(z=rank - 1)).wait_send()

                @pl.when(j < sent)
                def _(j=j):
                    t.copy(src.at[j, :, 0:WIDTH], dst.at[5 - sent + j], row_sems, (i, j), t.device(z=rank + 1)).wait_recv()

        def own_rows(src, dst, i, start, back=False):
            for j in range(5):
                @pl.when(j < 5 - sent)
                def _(j=j):
                    a, b = (place(j), j) if back else (j, place(j))
                    k = pltpu.make_async_copy(src.at[a, :, 0:WIDTH], dst.at[b, :, 0:WIDTH], r.loc_sem.at[i, j])
                    k.start() if start else k.wait()

        biases = [
            t.copy(r.bsh, r.bz.at[rank], (r.bias_send, r.bias_recv), d - 1, t.device(z=lax.rem(rank + d, 4))) for d in (1, 2, 3)
        ]
        t.barrier()
        own_rows(r.x_own, x_ref, 0, True)
        ag(groups[0], 0)
        for k in biases:
            k.start()
        rows_out(r.x_own, x_ref, 0)
        own_rows(r.dy_own, dy, 1, True)
        g[t.z, t.y, t.x, t.c] = r.wsh[...]
        r.bz[rank] = r.bsh[...]
    else:
        copies = [
            pltpu.make_async_copy(r.g_in, g, r.loc_sem.at[0, 0]),
            pltpu.make_async_copy(r.dy_own, dy, r.loc_sem.at[0, 1]),
            pltpu.make_async_copy(r.x_own, x_ref, r.loc_sem.at[0, 2]),
        ]
        for k in copies:
            k.start()
        for k in copies:
            k.wait()
    r.sums[...] = jnp.zeros_like(r.sums)
    r.six[...] = jnp.zeros_like(r.six)
    r.pad[...] = pad_lane(4 * ROWS)

    def first_norm(u):
        n, _s = normalize(x_ref[u].astype(F32))
        h2[u] = (n * vrow(0) + vrow(1)).astype(BF16)

    if comm:
        own_rows(r.x_own, x_ref, 0, False)

        @pl.loop(0, 5 - sent)
        def _(j):
            first_norm(place(j))

        ag(groups[0], 1)
        ag(groups[0], 2)
        ag(groups[1], 0)
        rows_in_wait(r.x_own, x_ref, 0)

        @pl.loop(0, got)
        def _(j):
            first_norm(got_at + j)

        for k in biases:
            k.wait()
        ag(groups[0], 3)
        ag(groups[1], 1)
        ag(groups[2], 0)
        ag(groups[0], 4)
    else:
        pl.loop(0, UNITS)(first_norm)

    def bias_pair(i):
        if i < 2:
            return jnp.concatenate([r.bz[2 * i, 1:2, 0:384], r.bz[2 * i + 1, 1:2, 0:384]], axis=1)
        parts = []
        for a in (0, 2):
            for o in range(3):
                parts += [r.bz[a + m, 1:2, 384 + 64 * o : 448 + 64 * o] for m in (0, 1)]
        return jnp.concatenate(parts, axis=1)

    def w_pair(i):
        if i < 2:
            return jnp.concatenate([weight(2 * i, group_a), weight(2 * i + 1, group_a)], axis=1)
        return wb[:, 0:768]

    def project(parts):
        @blocks
        def _(u0, count):
            h1 = rows_of(h2, u0, count)
            for i in parts:
                out = nn(h1, w_pair(i)) + bias_pair(i)
                qkv[u0 : u0 + count, :, 768 * i : 768 * (i + 1)] = out.astype(BF16).reshape(count, ROWS, 768)

    project((0, 1))
    if comm:
        ag(groups[1], 2)

    def pair_columns(ref, u0, count, p):
        return [
            ref[pl.ds(u0, count), :, pl.ds(pl.multiple_of(384 * p + 128 * i, 128), 128)].reshape(count * ROWS, 128)
            for i in range(3)
        ]

    def forward_images(parts, p):
        results = []
        for u0, count in parts:
            q, k, v = pair_columns(qkv, u0, count, p)
            results.append(attend_pair(q, k, v, r.pad[0 : count * ROWS]))
        for (u0, count), (out, logs) in zip(parts, results):
            att[u0 : u0 + count, :, pl.ds(pl.multiple_of(128 * p, 128), 128)] = out.reshape(count, ROWS, 128)
            old = rows_of(lse, u0, count)
            for h in (0, 1):
                old = jnp.where(lanes() == 2 * p + h, logs[h], old)
            put_rows(lse, u0, count, old)

    def images(some, p):
        pl.when(rank < 3)(lambda: some([(0, 4)], p))
        pl.when(rank == 2)(lambda: some([(4, 1)], p))
        pl.when(rank == 3)(lambda: some([(u, 1) for u in range(UNITS)], p))

    def ticks(p, steps):
        if comm:
            for at, functions in steps.items():
                @pl.when(p == at)
                def _(functions=functions):
                    for f in functions:
                        f()

    @pl.loop(0, 4)
    def _(p):
        images(forward_images, p)
        ticks(p, {
            0: [lambda: rows_out(r.dy_own, dy, 1)],
            1: [lambda: ag(groups[1], 3), lambda: ag(groups[2], 1)],
            2: [lambda: ag(groups[1], 4), lambda: ag(groups[2], 2), lambda: ag(groups[3], 0)],
        })

    def unpack_b():
        parts = [weight(z, group_b) for z in range(4)]
        o01 = [t[:, 0:128] for t in parts]
        qs, ks, vs, o2 = ([t[:, 128 + 64 * i : 192 + 64 * i] for t in parts] for i in range(4))
        cols = []
        for i in (0, 2):
            cols += [cat(qs[i], qs[i + 1]), cat(ks[i], ks[i + 1]), cat(vs[i], vs[i + 1])]
        cols += o01 + [cat(o2[0], o2[1]), cat(o2[2], o2[3])]
        for i, part in enumerate(cols):
            wb[:, 128 * i : 128 * (i + 1)] = part

    unpack_b()
    project((2,))

    @pl.loop(4, 6)
    def _(p):
        images(forward_images, p)
        ticks(p, {
            4: [lambda: ag(groups[2], 3), lambda: ag(groups[3], 1)],
            5: [lambda: ag(groups[2], 4), lambda: ag(groups[3], 2), lambda: ag(groups[4], 0)],
        })

    def middle_of(u0, count):
        return rows_of(x_ref, u0, count).astype(F32) + nt(rows_of(att, u0, count), wb[:, 768:1536]) + vrow(4)

    @blocks
    def _(u0, count):
        mid = middle_of(u0, count)
        n, _s = normalize(mid)
        put_rows(h2, u0, count, (n * vrow(2) + vrow(3)).astype(BF16))
        put_rows(y, u0, count, mid + vrow(5))
        put_rows(e, u0, count, jnp.zeros((count * ROWS, WIDTH), F32))

    if comm:
        own_rows(r.dy_own, dy, 1, False)
        rows_in_wait(r.dy_own, dy, 1)
        ag_sent(groups[2])

    @pl.loop(0, CHUNKS)
    def _(c):
        @pl.loop(0, 2)
        def _(zp):
            at = pl.multiple_of(768 + 512 * c, 128)
            ucols, dcols = pl.ds(at, 256), pl.ds(pl.multiple_of(at + 256, 128), 256)
            up = jnp.concatenate([weight(2 * zp, ucols), weight(2 * zp + 1, ucols)], axis=1)
            down = jnp.concatenate([weight(2 * zp, dcols), weight(2 * zp + 1, dcols)], axis=1)
            bcols = pl.ds(pl.multiple_of(256 * c, 128), 256)
            hb = jnp.concatenate([r.bz[2 * zp, 0:1, bcols], r.bz[2 * zp + 1, 0:1, bcols]], axis=1)

            @blocks
            def _(u0, count):
                u = nn(rows_of(h2, u0, count), up) + hb
                dz = nn(rows_of(dy, u0, count), down)
                big_phi, small_phi = gelu_terms(u)
                z = (u * big_phi).astype(BF16)
                du = (dz * (big_phi + small_phi)).astype(BF16)
                zdu[u0 : u0 + count, :, 0:512] = z.reshape(count, ROWS, 512)
                zdu[u0 : u0 + count, :, 512:1024] = du.reshape(count, ROWS, 512)
                r.six[2 * c + zp, 0:1, :] += column_sums(du.astype(F32))
                put_rows(y, u0, count, rows_of(y, u0, count) + nt(z, down))
                put_rows(e, u0, count, rows_of(e, u0, count) + nt(du, up))

            def at_step(cc, zz):
                return pl.when((c == cc) & (zp == zz))

            if comm:
                @at_step(0, 1)
                def _():
                    ag(groups[3], 4)
                    ag_sent(groups[3])
                    ag(groups[4], 2)

                @at_step(1, 0)
                def _():
                    ag(groups[4], 3)
                    rs(at_chunk(0), 1)

                pl.when((c > 0) & (zp == 1))(lambda: rs(at_chunk(c - 1), 2))
                at_step(2, 0)(lambda: rs(at_chunk(1), 1))

            @whole
            def _(count):
                h2v, dyv = rows_of(h2, 0, count), rows_of(dy, 0, count)
                gu = tn(h2v, zdu[0:count, :, 512:1024].reshape(count * ROWS, 512)).astype(BF16)
                gd = tn(dyv, zdu[0:count, :, 0:512].reshape(count * ROWS, 512)).astype(BF16)
                for i in range(2):
                    put_weight(2 * zp + i, ucols, gu[:, 256 * i : 256 * (i + 1)])
                    put_weight(2 * zp + i, dcols, gd[:, 256 * i : 256 * (i + 1)])

            if comm:
                @at_step(0, 0)
                def _():
                    ag(groups[3], 3)
                    ag(groups[4], 1)

                @at_step(1, 0)
                def _():
                    ag(groups[4], 4)
                    ag_sent(groups[4])

                at_step(2, 0)(lambda: rs(at_chunk(0), 4))

                @pl.when(zp == 1)
                def _():
                    pl.when(c > 0)(lambda: rs(at_chunk(c - 1), 3))
                    rs(at_chunk(c), 0)

    @blocks
    def _(u0, count):
        zdu[u0 : u0 + count, :, 0:768] = rows_of(y, u0, count).astype(BF16).reshape(count, ROWS, WIDTH)
        n, scale = normalize(middle_of(u0, count))
        grad = rows_of(e, u0, count)
        dyv = rows_of(dy, u0, count).astype(F32)
        dmid = dyv + norm_back(grad, vrow(2), n, scale)
        r.sums[2:3, :] += column_sums(grad * n)
        r.sums[3:4, :] += column_sums(grad)
        r.sums[4:5, :] += column_sums(dmid)
        r.sums[5:6, :] += column_sums(dyv)
        put_rows(e, u0, count, dmid)
        put_rows(h2, u0, count, dmid.astype(BF16))

    if comm:
        rs(at_chunk(2), 1)
        own_rows(zdu, r.yout, 2, True, True)
        rows_back(zdu, r.yout, 2)
        ag_sent(groups[0])
        ag_sent(groups[1])
    else:
        out_copy = pltpu.make_async_copy(zdu.at[:, :, 0:768], r.yout, r.loc_sem.at[0, 0])
        out_copy.start()

    @whole
    def _(count):
        go = tn(rows_of(h2, 0, count), rows_of(att, 0, count)).astype(BF16)
        for z in range(4):
            put_weight(z, slice(384, 512), go[:, 128 * z : 128 * (z + 1)])
            put_weight(z, slice(704, 768), go[:, 512 + 64 * z : 576 + 64 * z])

    @blocks
    def _(u0, count):
        d_att = nn(rows_of(h2, u0, count), wb[:, 768:1536]).astype(BF16)
        put_rows(dy, u0, count, d_att)
        prod = d_att.astype(F32) * rows_of(att, u0, count).astype(F32)
        high = prod.astype(BF16)
        feature, lane = (lax.broadcasted_iota(jnp.int32, (WIDTH, 128), i) for i in (0, 1))
        heads = jnp.where(feature // HEAD_DIM == lane, 1.0, 0.0).astype(BF16)
        dots = nn(high, heads) + nn((prod - high.astype(F32)).astype(BF16), heads)
        logs = jnp.where(lanes() < 12, rows_of(lse, u0, count), 0.0)
        terms = jnp.where(lanes() == 127, -1.0, 0.0)
        for i, part in enumerate(split_three(logs) + split_three(dots)):
            terms = terms + (part if i == 0 else pltpu.roll(part, 12 * i, axis=1))
        put_rows(r.terms, u0, count, (-terms).astype(BF16))

    if comm:
        rs(at_chunk(1), 4)

    def backward_images(parts, p):
        at = pl.ds(pl.multiple_of(128 * p, 128), 128)
        results = []
        for u0, count in parts:
            q, k, v = pair_columns(qkv, u0, count, p)
            grad = dy[u0 : u0 + count, :, at].reshape(count * ROWS, 128)
            results.append(attend_pair_back(q, k, v, grad, rows_of(r.terms, u0, count), 2 * p, r.pad[0 : count * ROWS]))
        for (u0, count), parts_out in zip(parts, results):
            for i, part in enumerate(parts_out):
                qkv[u0 : u0 + count, :, pl.ds(pl.multiple_of(384 * p + 128 * i, 128), 128)] = part.reshape(count, ROWS, 128)
            r.six[p, 1:2, 0:128] += column_sums(parts_out[0].astype(F32))
            r.six[p, 1:2, 128:256] += column_sums(parts_out[2].astype(F32))

    @pl.loop(4, 6)
    def _(p):
        images(backward_images, p)
        ticks(p, {
            4: [lambda: rs(at_chunk(2), 2)],
            5: [lambda: rs(at_chunk(2), 3)],
        })

    @blocks
    def _(u0, count):
        n, _s = normalize(rows_of(x_ref, u0, count).astype(F32))
        put_rows(h2, u0, count, (n * vrow(0) + vrow(1)).astype(BF16))

    def in_grads(count, i):
        gq = tn(rows_of(h2, 0, count), qkv[0:count, :, 768 * i : 768 * (i + 1)].reshape(count * ROWS, 768)).astype(BF16)
        if i < 2:
            put_weight(2 * i, group_a, gq[:, 0:384])
            put_weight(2 * i + 1, group_a, gq[:, 384:768])
        else:
            for z in range(4):
                base = 384 * (z // 2) + 64 * (z % 2)
                for o in range(3):
                    put_weight(z, slice(512 + 64 * o, 576 + 64 * o), gq[:, base + 128 * o : base + 128 * o + 64])

    whole(lambda count: in_grads(count, 2))
    if comm:
        rs(groups[1], 0)

    @pl.loop(0, 4)
    def _(p):
        images(backward_images, p)
        ticks(p, {
            0: [lambda: rs(groups[1], 1), lambda: rs(at_chunk(2), 4)],
            1: [lambda: rs(groups[1], 2)],
            2: [lambda: rs(groups[1], 3)],
            3: [lambda: rs(groups[1], 4)],
        })

    @blocks
    def _(u0, count):
        all_three = rows_of(qkv, u0, count)
        grad = nt(all_three[:, 0:768], w_pair(0))
        grad += nt(all_three[:, 768:1536], w_pair(1))
        grad += nt(all_three[:, 1536:2304], w_pair(2))
        put_rows(y, u0, count, grad)

    for i in range(2):
        whole(lambda count, i=i: in_grads(count, i))
    if comm:
        rs(groups[0], 0)
        own_rows(zdu, r.yout, 2, False, True)
        rows_back_wait(zdu, r.yout, 2)
    else:
        out_copy.wait()

    @blocks
    def _(u0, count):
        n, scale = normalize(rows_of(x_ref, u0, count).astype(F32))
        grad = rows_of(y, u0, count)
        r.sums[0:1, :] += column_sums(grad * n)
        r.sums[1:2, :] += column_sums(grad)
        out = rows_of(e, u0, count) + norm_back(grad, vrow(0), n, scale)
        zdu[u0 : u0 + count, :, 0:768] = out.astype(BF16).reshape(count, ROWS, WIDTH)

    for s in range(6):
        for i in range(2):
            hidden = 512 * s + 256 * i
            r.sums[6 + hidden // 768 : 7 + hidden // 768, hidden % 768 : hidden % 768 + 256] = r.six[s, 0:1, 256 * i : 256 * (i + 1)]
            r.sums[10 + i : 11 + i, 128 * s : 128 * (s + 1)] = r.six[s, 1:2, 128 * i : 128 * (i + 1)]

    if not comm:
        last_copies = [
            pltpu.make_async_copy(zdu.at[:, :, 0:768], r.gin, r.loc_sem.at[0, 0]),
            pltpu.make_async_copy(g, r.gout, r.loc_sem.at[0, 1]),
        ]
        for k in last_copies:
            k.start()
        for k in last_copies:
            k.wait()
        return

    own_rows(zdu, r.gin, 3, True, True)
    rows_back(zdu, r.gin, 3)

    def sum_step(slot, device):
        k = t.copy(r.sums, r.sum_in.at[slot], (r.sum_send, r.sum_recv), slot, device)
        k.start()
        return k

    for stage in range(3):
        k = sum_step(stage, t.partners()[stage])
        rs(groups[0], stage + 1)
        k.wait()
        r.sums[...] += r.sum_in[stage]
    steps = [sum_step(2 + d, t.device(z=lax.rem(rank + d, 4))) for d in (1, 2, 3)]
    rs(groups[0], 4)
    for k in steps:
        k.wait()
    r.total[...] = r.sums[...] + r.sum_in[3] + r.sum_in[4] + r.sum_in[5]
    own_rows(zdu, r.gin, 3, False, True)
    rows_back_wait(zdu, r.gin, 3)
    rows_out(r.x_own, x_ref, 0, True)
    rows_out(r.dy_own, dy, 1, True)


def run_kernel(comm, x, dy, weights, vectors, biases):
    vmem, hbm = pl.BlockSpec(memory_space=pltpu.VMEM), pl.BlockSpec(memory_space=pl.ANY)
    units, own = (UNITS, ROWS, WIDTH), (x.shape[0], ROWS, WIDTH)
    shape = jax.ShapeDtypeStruct
    sem = pltpu.SemaphoreType.DMA
    ins = ["x_own", "dy_own", "wsh" if comm else "g_in", "vec", "bsh" if comm else "bz"]
    in_specs = [hbm, hbm, vmem if comm else hbm, vmem, vmem]
    outs = {"yout": (shape(own, BF16), hbm), "gin": (shape(own, BF16), hbm)}
    if comm:
        outs |= {"gsh": (shape((96, COLS), F32), vmem), "total": (shape((16, WIDTH), F32), vmem)}
    else:
        outs |= {"gout": (shape((4, 2, 2, 2, 96, COLS), BF16), hbm), "sums": (shape((16, WIDTH), F32), vmem)}
    scratch = {
        "g": pltpu.VMEM((4, 2, 2, 2, 96, COLS), BF16),
        "wb": pltpu.VMEM((WIDTH, 1536), BF16),
        "x": pltpu.VMEM(units, BF16),
        "qkv": pltpu.VMEM((UNITS, ROWS, COLS), BF16),
        "att": pltpu.VMEM(units, BF16),
        "h2": pltpu.VMEM(units, BF16),
        "dy": pltpu.VMEM(units, BF16),
        "y": pltpu.VMEM(units, F32),
        "e": pltpu.VMEM(units, F32),
        "lse": pltpu.VMEM((UNITS, ROWS, 128), F32),
        "zdu": pltpu.VMEM((UNITS, ROWS, 1024), BF16),
        "terms": pltpu.VMEM((UNITS, ROWS, 128), BF16),
        "pad": pltpu.VMEM((4 * ROWS, 128), BF16),
        "six": pltpu.VMEM((6, 8, 512), F32),
        "loc_sem": sem((4, 5)),
    }
    if comm:
        scratch |= {
            "sums": pltpu.VMEM((16, WIDTH), F32),
            "sum_in": pltpu.VMEM((6, 16, WIDTH), F32),
            "bz": pltpu.VMEM((4, 8, WIDTH), F32),
            "rc": pltpu.VMEM((2, 4, 2, 2, 96, 512), BF16),
            "r2": pltpu.VMEM((2, 2, 4, 2, 48, 512), BF16),
            "r1": pltpu.VMEM((2, 2, 4, 48, 512), BF16),
            "rz": pltpu.VMEM((2, 3, 96, 512), BF16),
            "ag_send": sem((5, 8)), "ag_recv": sem((5, 8)),
            "rs_send": sem((5, 8)), "rs_recv": sem((5, 8)),
            "row_send": sem((4, 3)), "row_recv": sem((4, 3)),
            "bias_send": sem((3,)), "bias_recv": sem((3,)),
            "sum_send": sem((6,)), "sum_recv": sem((6,)),
        }
    params = dict(collective_id=0, has_side_effects=True) if comm else {}
    return pl.pallas_call(
        functools.partial(kernel, ins + list(outs) + list(scratch), comm),
        out_shape=[v[0] for v in outs.values()],
        in_specs=in_specs,
        out_specs=[v[1] for v in outs.values()],
        scratch_shapes=list(scratch.values()),
        compiler_params=pltpu.CompilerParams(vmem_limit_bytes=64 * 2**20 - 2**16, **params),
    )(x, dy, weights, vectors, biases)


def pack_shard(attention_in, attention_out, hidden_in, hidden_out):
    q, k, v = attention_in[:, 0] * 0.125, attention_in[:, 1], attention_in[:, 2]
    out_t, down_t = attention_out.T, hidden_out.T
    cols = [q[:, :128], k[:, :128], v[:, :128], out_t[:, :128], q[:, 128:], k[:, 128:], v[:, 128:], out_t[:, 128:]]
    for c in range(CHUNKS):
        cols += [hidden_in[:, 256 * c : 256 * (c + 1)], down_t[:, 256 * c : 256 * (c + 1)]]
    return jnp.concatenate([t.astype(BF16) for t in cols], axis=1)


def unpack_shard(grad):
    q = jnp.concatenate([grad[:, 0:128], grad[:, 512:576]], axis=1) * 0.125
    k = jnp.concatenate([grad[:, 128:256], grad[:, 576:640]], axis=1)
    v = jnp.concatenate([grad[:, 256:384], grad[:, 640:704]], axis=1)
    out_t = jnp.concatenate([grad[:, 384:512], grad[:, 704:768]], axis=1)
    up = jnp.concatenate([grad[:, 768 + 512 * c : 1024 + 512 * c] for c in range(CHUNKS)], axis=1)
    down = jnp.concatenate([grad[:, 1024 + 512 * c : 1280 + 512 * c] for c in range(CHUNKS)], axis=1)
    return jnp.stack([q, k, v], axis=1), out_t.T, up, down.T


def nesterov(weight_old, moment_old, average_old, gradient, rate, decay):
    step_dir = gradient + decay * weight_old
    moment_new = MOMENTUM * moment_old + step_dir
    weight_new = weight_old - rate * (step_dir + MOMENTUM * moment_new)
    return (weight_new, moment_new, AVERAGE * average_old + (1.0 - AVERAGE) * weight_new)


def local(
    tokens, cotangent, slot_live,
    vectors, vectors_momentum, vectors_average,
    column_bias, column_bias_momentum, column_bias_average,
    hidden_bias, hidden_bias_momentum, hidden_bias_average,
    attention_in, attention_in_momentum, attention_in_average,
    attention_out, attention_out_momentum, attention_out_average,
    hidden_in, hidden_in_momentum, hidden_in_average,
    hidden_out, hidden_out_momentum, hidden_out_average,
):
    rows_dev = tokens.shape[0]
    rank = lax.axis_index("mp")
    total_rows = rows_dev * lax.axis_size("mp") * lax.axis_size("dp")
    own_units = rows_dev // UNIT
    unit = rank * own_units + jnp.arange(own_units, dtype=jnp.int32)
    slot = jnp.where(unit < 4 * SLOT_L, unit // 4, unit - 3 * SLOT_L)
    live = jnp.sum(
        jnp.where(slot[:, None] == jnp.arange(slot_live.shape[1], dtype=jnp.int32)[None], slot_live, 0), axis=1
    ).astype(BF16)

    def in_units(rows):
        return jnp.pad(rows.reshape(own_units, UNIT, WIDTH), ((0, 0), (0, ROWS - UNIT), (0, 0)))

    def take(units, table):
        return jnp.take(units, jnp.array(table, jnp.int32)[rank], axis=0)

    def to_work(units):
        got = lax.ppermute(units[3:5], "mp", [(0, 1), (1, 2), (2, 3)])
        table = [[0, 1, 2, 3, 3, 3, 3], [0, 1, 2, 6, 6, 6, 6], [0, 1, 5, 6, 2, 2, 2], [0, 1, 2, 3, 4, 5, 6]]
        return take(jnp.concatenate([units, got], axis=0), table)

    def from_work(work):
        theirs = take(work, [[0, 0], [3, 3], [2, 3], [5, 6]])
        got = lax.ppermute(theirs, "mp", [(1, 0), (2, 1), (3, 2)])
        table = [[0, 1, 2, 3, 8], [0, 1, 2, 7, 8], [0, 1, 4, 7, 8], [0, 1, 2, 3, 4]]
        return take(jnp.concatenate([work, got], axis=0), table)[:, :UNIT].reshape(rows_dev, WIDTH)

    x, dy = in_units(tokens), in_units(cotangent) * live[:, None, None]
    shard = pack_shard(attention_in, attention_out, hidden_in, hidden_out)
    bq, bv = column_bias[0] * 0.125, column_bias[1]
    none = jnp.zeros((128,), F32)
    row = jnp.concatenate([bq[:128], none, bv[:128], bq[128:], none[:64], bv[128:], none, none[:64]])
    bias_rows = jnp.concatenate([hidden_bias[None], row[None], jnp.zeros((6, WIDTH), F32)], axis=0)

    if lax.axis_size("dp") == 8:
        yout, gin, reduced, total = run_kernel(True, x, dy, shard, vectors, bias_rows)
        block_output, input_gradient = (t[:, :UNIT].reshape(rows_dev, WIDTH) for t in (yout, gin))
    else:
        weights = lax.all_gather(lax.all_gather(shard, "dp", axis=0, tiled=True), "mp", axis=0)
        weights = weights.reshape(4, 2, 2, 2, 96, COLS)
        all_bias = lax.all_gather(bias_rows, "mp", axis=0)
        yout, gin, grads, total = run_kernel(False, to_work(x), to_work(dy), weights, vectors, all_bias)
        block_output, input_gradient = from_work(yout), from_work(gin)
        reduced = lax.psum_scatter(grads.reshape(4, WIDTH, COLS), "mp", scatter_dimension=0, tiled=True)[0]
        reduced = lax.psum_scatter(reduced, "dp", scatter_dimension=0, tiled=True).astype(F32)
        total = lax.psum(total, ("dp", "mp"))
    vector_grad = total[0:6]
    hidden_grad = jnp.transpose(total[6:10].reshape(CHUNKS, 2, 2, 256), (1, 2, 0, 3)).reshape(4, 768)
    hidden_grad = lax.dynamic_index_in_dim(hidden_grad, rank, 0, keepdims=False)
    pq, pv = total[10].reshape(PAIRS, 2, 64), total[11].reshape(PAIRS, 2, 64)

    def own_heads(pairs):
        second = pairs[4:6].reshape(4, 64)
        return jnp.concatenate(
            [lax.dynamic_index_in_dim(pairs, rank, 0, keepdims=False).reshape(128),
             lax.dynamic_index_in_dim(second, rank, 0, keepdims=False)]
        )

    column_grad = jnp.stack([own_heads(pq) * 0.125, own_heads(pv)])
    gqkv, gout, gup, gdown = unpack_shard(reduced)
    root = math.sqrt(total_rows)
    steps = (
        (vectors, vectors_momentum, vectors_average, vector_grad, RATE_VECTORS, 0.0),
        (column_bias, column_bias_momentum, column_bias_average, column_grad, RATE_COLUMN, 0.0),
        (hidden_bias, hidden_bias_momentum, hidden_bias_average, hidden_grad, RATE_HIDDEN, 0.0),
        (attention_in, attention_in_momentum, attention_in_average, gqkv, RATE_ATTENTION_IN, DECAY),
        (attention_out, attention_out_momentum, attention_out_average, gout, RATE_ATTENTION_OUT, DECAY),
        (hidden_in, hidden_in_momentum, hidden_in_average, gup, RATE_HIDDEN_IN, DECAY),
        (hidden_out, hidden_out_momentum, hidden_out_average, gdown, RATE_HIDDEN_OUT, DECAY),
    )
    outs = [block_output, input_gradient]
    for weight, moment, average, gradient, rate, decay in steps:
        outs.extend(nesterov(weight, moment, average, gradient, rate / root, decay))
    return tuple(outs)


def solution(mesh):
    rows, matrix, side = P(("dp", "mp"), None), P("dp", None, "mp"), P("mp", "dp")
    params = [P()] * 3 + [P(None, "mp")] * 3 + [P("mp")] * 3 + [matrix] * 3 + [side] * 3 + [P("dp", "mp")] * 3 + [side] * 3
    return jax.shard_map(
        local,
        mesh=mesh,
        in_specs=(rows, rows, P("dp", None), *params),
        out_specs=(rows, rows, *params),
        check_vma=False,
    )
```

```python
import functools
import math
import types

import jax
import jax.numpy as jnp
from jax import lax
from jax.experimental import pallas as pl
from jax.experimental.pallas import tpu as pltpu
from jax.sharding import PartitionSpec as P

F32, BF16 = jnp.float32, jnp.bfloat16
WIDTH = 768
HEAD_DIM = 64
PATCH_L = 784
PATCH_S = 196
SLOT_L = 3
SLOT_S = 8
UNIT = 196
ROWS = 208
UNITS = 7
PAIRS = 6
CHUNKS = 3
COLS = 2304

EPSILON = 1e-06
MOMENTUM = 0.9
AVERAGE = 0.8
DECAY = 0.0001
RATE_VECTORS = 0.06
RATE_COLUMN = 0.01
RATE_HIDDEN = 0.4
RATE_ATTENTION_IN = 0.005
RATE_ATTENTION_OUT = 0.5
RATE_HIDDEN_IN = 0.05
RATE_HIDDEN_OUT = 0.015


def nn(a, b):
    return lax.dot_general(a, b, (((1,), (0,)), ((), ())), preferred_element_type=F32)


def nt(a, b):
    return lax.dot_general(a, b, (((1,), (1,)), ((), ())), preferred_element_type=F32)


def tn(a, b):
    return lax.dot_general(a, b, (((0,), (0,)), ((), ())), preferred_element_type=F32)


def normalize(values):
    centred = values - jnp.mean(values, axis=-1, keepdims=True)
    spread = jnp.mean(centred * centred, axis=-1, keepdims=True)
    scale = lax.rsqrt(spread + EPSILON)
    return centred * scale, scale


def norm_back(cotangent, gain, n, scale):
    cg = cotangent * gain
    return scale * (
        cg - jnp.mean(cg, axis=-1, keepdims=True) - n * jnp.mean(cg * n, axis=-1, keepdims=True)
    )


def column_sums(values):
    return jnp.sum(values, axis=0, keepdims=True)


def split_three(values):
    high = values.astype(BF16).astype(F32)
    mid = (values - high).astype(BF16).astype(F32)
    return high, mid, values - high - mid


def gelu_terms(u):
    e = jnp.exp(u * u * -0.5)
    k = 1.0 / (1.0 + jnp.abs(u) * (0.3275911 * math.sqrt(0.5)))
    poly = k * (
        0.5 * 0.254829592
        + k * (0.5 * -0.284496736 + k * (0.5 * 1.421413741 + k * (0.5 * -1.453152027 + k * (0.5 * 1.061405429))))
    )
    tail = poly * e
    big_phi = jnp.where(u < 0.0, tail, 1.0 - tail)
    return big_phi, u * e * (1.0 / math.sqrt(2.0 * math.pi))


def rows_of(ref, u0, count):
    return ref[u0 : u0 + count].reshape(count * ROWS, ref.shape[-1])


def put_rows(ref, u0, count, value):
    ref[u0 : u0 + count] = value.reshape(count, ROWS, value.shape[-1])


def lanes():
    return lax.broadcasted_iota(jnp.int32, (1, 128), 1)


def pad_lane(rows):
    at = lax.broadcasted_iota(jnp.int32, (rows, 128), 0)
    lane = lax.broadcasted_iota(jnp.int32, (rows, 128), 1)
    return jnp.where((lax.rem(at, ROWS) >= UNIT) & (lane == 127), -1e30, 0.0).astype(BF16)


def own_lanes(values, h):
    mask = jnp.where((lanes() < 64) == (h == 0), 1.0, 0.0).astype(BF16)
    return values * mask


def cat(*parts):
    return jnp.concatenate(parts, axis=1)


def one_lanes(*which):
    hit = functools.reduce(jnp.logical_or, [lanes() == w for w in which])
    return jnp.where(hit, 1.0, 0.0).astype(BF16)


def attend_pair(q, k, v, pad):
    keys = cat(k, pad)
    ones = jnp.broadcast_to(one_lanes(127), (q.shape[0], 128))
    outs, logs = [], []
    for h in (0, 1):
        s = nt(cat(own_lanes(q, h), ones), keys)
        top = jnp.max(s, axis=-1, keepdims=True)
        e = jnp.exp(s - top)
        total = jnp.sum(e, axis=-1, keepdims=True)
        outs.append(nn(e.astype(BF16), v) * (1.0 / total))
        logs.append(top + jnp.log(total))
    return jnp.where(lanes() < 64, outs[0], outs[1]).astype(BF16), logs


def attend_pair_back(q, k, v, g, terms, first_head, pad):
    dq, dk, dv = [], [], []
    for h in (0, 1):
        i = first_head + h
        keys = cat(k, pad + one_lanes(i, 12 + i, 24 + i))
        values = cat(v, jnp.broadcast_to(one_lanes(36 + i, 48 + i, 60 + i), v.shape))
        p = jnp.exp(nt(cat(own_lanes(q, h), terms), keys))
        dp = nt(cat(own_lanes(g, h), terms), values)
        ds = (p * dp).astype(BF16)
        dv.append(tn(p.astype(BF16), g))
        dq.append(nn(ds, k))
        dk.append(tn(ds, q))
    left = lanes() < 64
    return [jnp.where(left, t[0], t[1]).astype(BF16) for t in (dq, dk, dv)]


class Sends:
    def __init__(self, r):
        self.r = r
        self.dp, self.z = lax.axis_index("dp"), lax.axis_index("mp")
        self.y, self.x, self.c = self.dp // 4, lax.rem(self.dp // 2, 2), lax.rem(self.dp, 2)

    def device(self, y=None, x=None, c=None, z=None):
        y, x, c, z = (own if new is None else new for own, new in ((self.y, y), (self.x, x), (self.c, c), (self.z, z)))
        return (4 * y + 2 * x + c, z)

    def copy(self, src, dst, sems, index, device):
        send, recv = sems
        return pltpu.make_async_remote_copy(
            src_ref=src, dst_ref=dst, send_sem=send.at[index], recv_sem=recv.at[index],
            device_id=device, device_id_type=pl.DeviceIdType.MESH,
        )

    def partners(self):
        return [self.device(c=1 - self.c), self.device(x=1 - self.x), self.device(y=1 - self.y)] + [
            self.device(z=lax.rem(self.z + d, 4)) for d in (1, 2, 3)
        ]

    def barrier(self):
        sem = pltpu.get_barrier_semaphore()
        for device in self.partners():
            pl.semaphore_signal(sem, inc=1, device_id=device, device_id_type=pl.DeviceIdType.MESH)
        pl.semaphore_wait(sem, 6)

    def gather(self, group, cols, stage):
        r, y, x, c, z = self.r, self.y, self.x, self.c, self.z
        sems = (r.ag_send, r.ag_recv)
        if stage == 0:
            return [
                self.copy(r.wsh.at[:, cols], r.g.at[z, y, x, c, :, cols], sems, (group, d - 1), self.device(z=lax.rem(z + d, 4)))
                for d in (1, 2, 3)
            ]
        if stage == 1:
            a, b = r.g.at[:, y, x, c, 0:48, cols], r.g.at[:, y, x, c, 48:96, cols]
            return [
                self.copy(a, a, sems, (group, 3), self.device(x=1 - x)),
                self.copy(b, b, sems, (group, 4), self.device(y=1 - y)),
            ]
        if stage == 2:
            a, b = r.g.at[:, y, :, c, 0:48, cols], r.g.at[:, :, x, c, 48:96, cols]
            return [
                self.copy(a, a, sems, (group, 5), self.device(y=1 - y)),
                self.copy(b, b, sems, (group, 6), self.device(x=1 - x)),
            ]
        a = r.g.at[:, :, :, c, :, cols]
        return [self.copy(a, a, sems, (group, 7), self.device(c=1 - c))]

    def scatter(self, group, cols, stage, bufs):
        r, y, x, c, z = self.r, self.y, self.x, self.c, self.z
        sems = (r.rs_send, r.rs_recv)
        rc, r2, r1, rz = bufs
        if stage == 0:
            return [self.copy(r.g.at[:, :, :, 1 - c, :, cols], rc, sems, (group, 0), self.device(c=1 - c))]
        if stage == 1:
            return [
                self.copy(r.g.at[:, 1 - y, :, c, 0:48, cols], r2.at[0], sems, (group, 1), self.device(y=1 - y)),
                self.copy(r.g.at[:, :, 1 - x, c, 48:96, cols], r2.at[1], sems, (group, 2), self.device(x=1 - x)),
            ]
        if stage == 2:
            return [
                self.copy(r.g.at[:, y, 1 - x, c, 0:48, cols], r1.at[0], sems, (group, 3), self.device(x=1 - x)),
                self.copy(r.g.at[:, 1 - y, x, c, 48:96, cols], r1.at[1], sems, (group, 4), self.device(y=1 - y)),
            ]
        return [
            self.copy(
                r.g.at[lax.rem(z + d, 4), y, x, c, :, cols], rz.at[d - 1], sems, (group, 4 + d), self.device(z=lax.rem(z + d, 4))
            )
            for d in (1, 2, 3)
        ]

    def add_up(self, cols, stage, bufs):
        r, y, x, c, z = self.r, self.y, self.x, self.c, self.z
        rc, r2, r1, rz = bufs

        def add(index, part):
            r.g[index] = r.g[index] + part

        every = slice(None)
        if stage < 3:
            @pl.loop(0, 4)
            def _(m):
                if stage == 0:
                    for i in range(2):
                        add((m, i, every, c, every, cols), rc[m, i])
                elif stage == 1:
                    add((m, y, every, c, slice(0, 48), cols), r2[0, m])
                    add((m, every, x, c, slice(48, 96), cols), r2[1, m])
                else:
                    add((m, y, x, c, slice(0, 48), cols), r1[0, m])
                    add((m, y, x, c, slice(48, 96), cols), r1[1, m])
        else:
            total = r.g[z, y, x, c, :, cols].astype(F32)
            for d in range(3):
                total = total + rz[d].astype(F32)
            r.gsh[:, cols] = total


def kernel(names, comm, *refs):
    r = types.SimpleNamespace(**dict(zip(names, refs)))
    g, wb, qkv, att, h2, dy, y, e, lse, zdu, x_ref = r.g, r.wb, r.qkv, r.att, r.h2, r.dy, r.y, r.e, r.lse, r.zdu, r.x
    rank = lax.axis_index("mp")

    def blocks(f):
        pl.when(rank != 2)(lambda: f(0, 4))
        pl.when(rank == 2)(lambda: f(0, 5))
        pl.when(rank == 3)(lambda: f(4, 3))

    def whole(f):
        pl.when(rank < 2)(lambda: f(4))
        pl.when(rank == 2)(lambda: f(5))
        pl.when(rank == 3)(lambda: f(7))

    vrow = lambda i: r.vec[i : i + 1, :]

    def weight(z, cols):
        return g[z, :, :, :, :, cols].reshape(WIDTH, -1)

    def put_weight(z, cols, value):
        g[z, :, :, :, :, cols] = value.reshape(2, 2, 2, 96, value.shape[-1])

    group_a, group_b = slice(0, 384), slice(384, 768)

    def chunk(c):
        return pl.ds(pl.multiple_of(768 + 512 * c, 128), 512)

    if comm:
        t = Sends(r)
        groups = [(0, group_a), (1, group_b)] + [(2 + c, chunk(c)) for c in range(CHUNKS)]
        at_chunk = lambda c: (2 + c, chunk(c))

        def ag(group, stage):
            if stage > 0:
                for k in t.gather(*group, stage - 1):
                    k.wait_recv()
            if stage < 4:
                for k in t.gather(*group, stage):
                    k.start()

        def ag_sent(group):
            for stage in range(4):
                for k in t.gather(*group, stage):
                    k.wait_send()

        def bufs(group):
            index, cols = group
            width = cols.size if isinstance(cols, pl.Slice) else cols.stop - cols.start
            turn = lax.rem(index, 2) if isinstance(index, jax.Array) else index % 2
            part = slice(0, width)
            return (
                r.rc.at[turn, :, :, :, :, part], r.r2.at[turn, :, :, :, :, part],
                r.r1.at[turn, :, :, :, part], r.rz.at[turn, :, :, part],
            )

        def rs(group, stage):
            b = bufs(group)
            if stage > 0:
                for k in t.scatter(*group, stage - 1, b):
                    k.wait()
                t.add_up(group[1], stage - 1, b)
            if stage < 4:
                for k in t.scatter(*group, stage, b):
                    k.start()

        sent = jnp.where(rank == 0, 1, jnp.where(rank == 3, 0, 2))
        got = jnp.where(rank == 0, 0, jnp.where(rank == 1, 1, 2))
        got_at = jnp.where(rank == 1, 3, jnp.where(rank == 2, 2, 5))
        theirs_at = jnp.where(rank == 0, 3, jnp.where(rank == 1, 2, 5))
        row_sems = (r.row_send, r.row_recv)

        def place(j):
            return jnp.where((rank == 2) & (j == 2), 4, j)

        def rows_out(src, dst, i, wait=False):
            for j in range(2):
                @pl.when(j < sent)
                def _(j=j):
                    k = t.copy(src.at[5 - sent + j], dst.at[theirs_at + j], row_sems, (i, j), t.device(z=rank + 1))
                    k.wait_send() if wait else k.start()

        def rows_in_wait(src, dst, i):
            for j in range(2):
                @pl.when(j < got)
                def _(j=j):
                    t.copy(src.at[j], dst.at[got_at + j], row_sems, (i, j), t.device(z=rank - 1)).wait_recv()

        def rows_back(src, dst, i):
            for j in range(2):
                @pl.when(j < got)
                def _(j=j):
                    t.copy(src.at[got_at + j, :, 0:WIDTH], dst.at[5 - got + j], row_sems, (i, j), t.device(z=rank - 1)).start()

        def rows_back_wait(src, dst, i):
            for j in range(2):
                @pl.when(j < got)
                def _(j=j):
                    t.copy(src.at[got_at + j, :, 0:WIDTH], dst.at[5 - got + j], row_sems, (i, j), t.device(z=rank - 1)).wait_send()

                @pl.when(j < sent)
                def _(j=j):
                    t.copy(src.at[j, :, 0:WIDTH], dst.at[5 - sent + j], row_sems, (i, j), t.device(z=rank + 1)).wait_recv()

        def own_rows(src, dst, i, start, back=False):
            for j in range(5):
                @pl.when(j < 5 - sent)
                def _(j=j):
                    a, b = (place(j), j) if back else (j, place(j))
                    k = pltpu.make_async_copy(src.at[a, :, 0:WIDTH], dst.at[b, :, 0:WIDTH], r.loc_sem.at[i, j])
                    k.start() if start else k.wait()

        biases = [
            t.copy(r.bsh, r.bz.at[rank], (r.bias_send, r.bias_recv), d - 1, t.device(z=lax.rem(rank + d, 4))) for d in (1, 2, 3)
        ]
        t.barrier()
        own_rows(r.x_own, x_ref, 0, True)
        ag(groups[0], 0)
        for k in biases:
            k.start()
        rows_out(r.x_own, x_ref, 0)
        own_rows(r.dy_own, dy, 1, True)
        g[t.z, t.y, t.x, t.c] = r.wsh[...]
        r.bz[rank] = r.bsh[...]
    else:
        copies = [
            pltpu.make_async_copy(r.g_in, g, r.loc_sem.at[0, 0]),
            pltpu.make_async_copy(r.dy_own, dy, r.loc_sem.at[0, 1]),
            pltpu.make_async_copy(r.x_own, x_ref, r.loc_sem.at[0, 2]),
        ]
        for k in copies:
            k.start()
        for k in copies:
            k.wait()
    r.sums[...] = jnp.zeros_like(r.sums)
    r.six[...] = jnp.zeros_like(r.six)
    r.pad[...] = pad_lane(4 * ROWS)

    def first_norm(u):
        n, _s = normalize(x_ref[u].astype(F32))
        h2[u] = (n * vrow(0) + vrow(1)).astype(BF16)

    if comm:
        own_rows(r.x_own, x_ref, 0, False)

        @pl.loop(0, 5 - sent)
        def _(j):
            first_norm(place(j))

        ag(groups[0], 1)
        ag(groups[0], 2)
        ag(groups[1], 0)
        rows_in_wait(r.x_own, x_ref, 0)

        @pl.loop(0, got)
        def _(j):
            first_norm(got_at + j)

        for k in biases:
            k.wait()
        ag(groups[0], 3)
        ag(groups[1], 1)
        ag(groups[2], 0)
        ag(groups[0], 4)
    else:
        pl.loop(0, UNITS)(first_norm)

    def bias_pair(i):
        if i < 2:
            return jnp.concatenate([r.bz[2 * i, 1:2, 0:384], r.bz[2 * i + 1, 1:2, 0:384]], axis=1)
        parts = []
        for a in (0, 2):
            for o in range(3):
                parts += [r.bz[a + m, 1:2, 384 + 64 * o : 448 + 64 * o] for m in (0, 1)]
        return jnp.concatenate(parts, axis=1)

    def w_pair(i):
        if i < 2:
            return jnp.concatenate([weight(2 * i, group_a), weight(2 * i + 1, group_a)], axis=1)
        return wb[:, 0:768]

    def project(parts):
        @blocks
        def _(u0, count):
            h1 = rows_of(h2, u0, count)
            for i in parts:
                out = nn(h1, w_pair(i)) + bias_pair(i)
                qkv[u0 : u0 + count, :, 768 * i : 768 * (i + 1)] = out.astype(BF16).reshape(count, ROWS, 768)

    project((0, 1))
    if comm:
        ag(groups[1], 2)

    def pair_columns(ref, u0, count, p):
        return [
            ref[pl.ds(u0, count), :, pl.ds(pl.multiple_of(384 * p + 128 * i, 128), 128)].reshape(count * ROWS, 128)
            for i in range(3)
        ]

    def forward_images(parts, p):
        results = []
        for u0, count in parts:
            q, k, v = pair_columns(qkv, u0, count, p)
            results.append(attend_pair(q, k, v, r.pad[0 : count * ROWS]))
        for (u0, count), (out, logs) in zip(parts, results):
            att[u0 : u0 + count, :, pl.ds(pl.multiple_of(128 * p, 128), 128)] = out.reshape(count, ROWS, 128)
            old = rows_of(lse, u0, count)
            for h in (0, 1):
                old = jnp.where(lanes() == 2 * p + h, logs[h], old)
            put_rows(lse, u0, count, old)

    def images(some, p):
        pl.when(rank < 3)(lambda: some([(0, 4)], p))
        pl.when(rank == 2)(lambda: some([(4, 1)], p))
        pl.when(rank == 3)(lambda: some([(u, 1) for u in range(UNITS)], p))

    def ticks(p, steps):
        if comm:
            for at, functions in steps.items():
                @pl.when(p == at)
                def _(functions=functions):
                    for f in functions:
                        f()

    @pl.loop(0, 4)
    def _(p):
        images(forward_images, p)
        ticks(p, {
            0: [lambda: rows_out(r.dy_own, dy, 1)],
            1: [lambda: ag(groups[1], 3), lambda: ag(groups[2], 1)],
            2: [lambda: ag(groups[1], 4), lambda: ag(groups[2], 2), lambda: ag(groups[3], 0)],
        })

    def unpack_b():
        parts = [weight(z, group_b) for z in range(4)]
        o01 = [t[:, 0:128] for t in parts]
        qs, ks, vs, o2 = ([t[:, 128 + 64 * i : 192 + 64 * i] for t in parts] for i in range(4))
        cols = []
        for i in (0, 2):
            cols += [cat(qs[i], qs[i + 1]), cat(ks[i], ks[i + 1]), cat(vs[i], vs[i + 1])]
        cols += o01 + [cat(o2[0], o2[1]), cat(o2[2], o2[3])]
        for i, part in enumerate(cols):
            wb[:, 128 * i : 128 * (i + 1)] = part

    unpack_b()
    project((2,))

    @pl.loop(4, 6)
    def _(p):
        images(forward_images, p)
        ticks(p, {
            4: [lambda: ag(groups[2], 3), lambda: ag(groups[3], 1)],
            5: [lambda: ag(groups[2], 4), lambda: ag(groups[3], 2), lambda: ag(groups[4], 0)],
        })

    def middle_of(u0, count):
        return rows_of(x_ref, u0, count).astype(F32) + nt(rows_of(att, u0, count), wb[:, 768:1536]) + vrow(4)

    @blocks
    def _(u0, count):
        mid = middle_of(u0, count)
        n, _s = normalize(mid)
        put_rows(h2, u0, count, (n * vrow(2) + vrow(3)).astype(BF16))
        put_rows(y, u0, count, mid + vrow(5))
        put_rows(e, u0, count, jnp.zeros((count * ROWS, WIDTH), F32))

    if comm:
        own_rows(r.dy_own, dy, 1, False)
        rows_in_wait(r.dy_own, dy, 1)
        ag_sent(groups[2])

    @pl.loop(0, CHUNKS)
    def _(c):
        @pl.loop(0, 2)
        def _(zp):
            at = pl.multiple_of(768 + 512 * c, 128)
            ucols, dcols = pl.ds(at, 256), pl.ds(pl.multiple_of(at + 256, 128), 256)
            up = jnp.concatenate([weight(2 * zp, ucols), weight(2 * zp + 1, ucols)], axis=1)
            down = jnp.concatenate([weight(2 * zp, dcols), weight(2 * zp + 1, dcols)], axis=1)
            bcols = pl.ds(pl.multiple_of(256 * c, 128), 256)
            hb = jnp.concatenate([r.bz[2 * zp, 0:1, bcols], r.bz[2 * zp + 1, 0:1, bcols]], axis=1)

            @blocks
            def _(u0, count):
                u = nn(rows_of(h2, u0, count), up) + hb
                dz = nn(rows_of(dy, u0, count), down)
                big_phi, small_phi = gelu_terms(u)
                z = (u * big_phi).astype(BF16)
                du = (dz * (big_phi + small_phi)).astype(BF16)
                zdu[u0 : u0 + count, :, 0:512] = z.reshape(count, ROWS, 512)
                zdu[u0 : u0 + count, :, 512:1024] = du.reshape(count, ROWS, 512)
                r.six[2 * c + zp, 0:1, :] += column_sums(du.astype(F32))
                put_rows(y, u0, count, rows_of(y, u0, count) + nt(z, down))
                put_rows(e, u0, count, rows_of(e, u0, count) + nt(du, up))

            def at_step(cc, zz):
                return pl.when((c == cc) & (zp == zz))

            if comm:
                @at_step(0, 1)
                def _():
                    ag(groups[3], 4)
                    ag_sent(groups[3])
                    ag(groups[4], 2)

                @at_step(1, 0)
                def _():
                    ag(groups[4], 3)
                    rs(at_chunk(0), 1)

                pl.when((c > 0) & (zp == 1))(lambda: rs(at_chunk(c - 1), 2))
                at_step(2, 0)(lambda: rs(at_chunk(1), 1))

            @whole
            def _(count):
                h2v, dyv = rows_of(h2, 0, count), rows_of(dy, 0, count)
                gu = tn(h2v, zdu[0:count, :, 512:1024].reshape(count * ROWS, 512)).astype(BF16)
                gd = tn(dyv, zdu[0:count, :, 0:512].reshape(count * ROWS, 512)).astype(BF16)
                for i in range(2):
                    put_weight(2 * zp + i, ucols, gu[:, 256 * i : 256 * (i + 1)])
                    put_weight(2 * zp + i, dcols, gd[:, 256 * i : 256 * (i + 1)])

            if comm:
                @at_step(0, 0)
                def _():
                    ag(groups[3], 3)
                    ag(groups[4], 1)

                @at_step(1, 0)
                def _():
                    ag(groups[4], 4)
                    ag_sent(groups[4])

                at_step(2, 0)(lambda: rs(at_chunk(0), 4))

                @pl.when(zp == 1)
                def _():
                    pl.when(c > 0)(lambda: rs(at_chunk(c - 1), 3))
                    rs(at_chunk(c), 0)

    @blocks
    def _(u0, count):
        zdu[u0 : u0 + count, :, 0:768] = rows_of(y, u0, count).astype(BF16).reshape(count, ROWS, WIDTH)
        n, scale = normalize(middle_of(u0, count))
        grad = rows_of(e, u0, count)
        dyv = rows_of(dy, u0, count).astype(F32)
        dmid = dyv + norm_back(grad, vrow(2), n, scale)
        r.sums[2:3, :] += column_sums(grad * n)
        r.sums[3:4, :] += column_sums(grad)
        r.sums[4:5, :] += column_sums(dmid)
        r.sums[5:6, :] += column_sums(dyv)
        put_rows(e, u0, count, dmid)
        put_rows(h2, u0, count, dmid.astype(BF16))

    if comm:
        rs(at_chunk(2), 1)
        own_rows(zdu, r.yout, 2, True, True)
        rows_back(zdu, r.yout, 2)
        ag_sent(groups[0])
        ag_sent(groups[1])
    else:
        out_copy = pltpu.make_async_copy(zdu.at[:, :, 0:768], r.yout, r.loc_sem.at[0, 0])
        out_copy.start()

    @whole
    def _(count):
        go = tn(rows_of(h2, 0, count), rows_of(att, 0, count)).astype(BF16)
        for z in range(4):
            put_weight(z, slice(384, 512), go[:, 128 * z : 128 * (z + 1)])
            put_weight(z, slice(704, 768), go[:, 512 + 64 * z : 576 + 64 * z])

    @blocks
    def _(u0, count):
        d_att = nn(rows_of(h2, u0, count), wb[:, 768:1536]).astype(BF16)
        put_rows(dy, u0, count, d_att)
        prod = d_att.astype(F32) * rows_of(att, u0, count).astype(F32)
        high = prod.astype(BF16)
        feature, lane = (lax.broadcasted_iota(jnp.int32, (WIDTH, 128), i) for i in (0, 1))
        heads = jnp.where(feature // HEAD_DIM == lane, 1.0, 0.0).astype(BF16)
        dots = nn(high, heads) + nn((prod - high.astype(F32)).astype(BF16), heads)
        logs = jnp.where(lanes() < 12, rows_of(lse, u0, count), 0.0)
        terms = jnp.where(lanes() == 127, -1.0, 0.0)
        for i, part in enumerate(split_three(logs) + split_three(dots)):
            terms = terms + (part if i == 0 else pltpu.roll(part, 12 * i, axis=1))
        put_rows(r.terms, u0, count, (-terms).astype(BF16))

    if comm:
        rs(at_chunk(1), 4)

    def backward_images(parts, p):
        at = pl.ds(pl.multiple_of(128 * p, 128), 128)
        results = []
        for u0, count in parts:
            q, k, v = pair_columns(qkv, u0, count, p)
            grad = dy[u0 : u0 + count, :, at].reshape(count * ROWS, 128)
            results.append(attend_pair_back(q, k, v, grad, rows_of(r.terms, u0, count), 2 * p, r.pad[0 : count * ROWS]))
        for (u0, count), parts_out in zip(parts, results):
            for i, part in enumerate(parts_out):
                qkv[u0 : u0 + count, :, pl.ds(pl.multiple_of(384 * p + 128 * i, 128), 128)] = part.reshape(count, ROWS, 128)
            r.six[p, 1:2, 0:128] += column_sums(parts_out[0].astype(F32))
            r.six[p, 1:2, 128:256] += column_sums(parts_out[2].astype(F32))

    @pl.loop(4, 6)
    def _(p):
        images(backward_images, p)
        ticks(p, {
            4: [lambda: rs(at_chunk(2), 2)],
            5: [lambda: rs(at_chunk(2), 3)],
        })

    @blocks
    def _(u0, count):
        n, _s = normalize(rows_of(x_ref, u0, count).astype(F32))
        put_rows(h2, u0, count, (n * vrow(0) + vrow(1)).astype(BF16))

    def in_grads(count, i):
        gq = tn(rows_of(h2, 0, count), qkv[0:count, :, 768 * i : 768 * (i + 1)].reshape(count * ROWS, 768)).astype(BF16)
        if i < 2:
            put_weight(2 * i, group_a, gq[:, 0:384])
            put_weight(2 * i + 1, group_a, gq[:, 384:768])
        else:
            for z in range(4):
                base = 384 * (z // 2) + 64 * (z % 2)
                for o in range(3):
                    put_weight(z, slice(512 + 64 * o, 576 + 64 * o), gq[:, base + 128 * o : base + 128 * o + 64])

    whole(lambda count: in_grads(count, 2))
    if comm:
        rs(groups[1], 0)

    @pl.loop(0, 4)
    def _(p):
        images(backward_images, p)
        ticks(p, {
            0: [lambda: rs(groups[1], 1), lambda: rs(at_chunk(2), 4)],
            1: [lambda: rs(groups[1], 2)],
            2: [lambda: rs(groups[1], 3)],
            3: [lambda: rs(groups[1], 4)],
        })

    @blocks
    def _(u0, count):
        all_three = rows_of(qkv, u0, count)
        grad = nt(all_three[:, 0:768], w_pair(0))
        grad += nt(all_three[:, 768:1536], w_pair(1))
        grad += nt(all_three[:, 1536:2304], w_pair(2))
        put_rows(y, u0, count, grad)

    for i in range(2):
        whole(lambda count, i=i: in_grads(count, i))
    if comm:
        rs(groups[0], 0)
        own_rows(zdu, r.yout, 2, False, True)
        rows_back_wait(zdu, r.yout, 2)
    else:
        out_copy.wait()

    @blocks
    def _(u0, count):
        n, scale = normalize(rows_of(x_ref, u0, count).astype(F32))
        grad = rows_of(y, u0, count)
        r.sums[0:1, :] += column_sums(grad * n)
        r.sums[1:2, :] += column_sums(grad)
        out = rows_of(e, u0, count) + norm_back(grad, vrow(0), n, scale)
        zdu[u0 : u0 + count, :, 0:768] = out.astype(BF16).reshape(count, ROWS, WIDTH)

    for s in range(6):
        for i in range(2):
            hidden = 512 * s + 256 * i
            r.sums[6 + hidden // 768 : 7 + hidden // 768, hidden % 768 : hidden % 768 + 256] = r.six[s, 0:1, 256 * i : 256 * (i + 1)]
            r.sums[10 + i : 11 + i, 128 * s : 128 * (s + 1)] = r.six[s, 1:2, 128 * i : 128 * (i + 1)]

    if not comm:
        last_copies = [
            pltpu.make_async_copy(zdu.at[:, :, 0:768], r.gin, r.loc_sem.at[0, 0]),
            pltpu.make_async_copy(g, r.gout, r.loc_sem.at[0, 1]),
        ]
        for k in last_copies:
            k.start()
        for k in last_copies:
            k.wait()
        return

    own_rows(zdu, r.gin, 3, True, True)
    rows_back(zdu, r.gin, 3)

    def sum_step(slot, device):
        k = t.copy(r.sums, r.sum_in.at[slot], (r.sum_send, r.sum_recv), slot, device)
        k.start()
        return k

    for stage in range(3):
        k = sum_step(stage, t.partners()[stage])
        rs(groups[0], stage + 1)
        k.wait()
        r.sums[...] += r.sum_in[stage]
    steps = [sum_step(2 + d, t.device(z=lax.rem(rank + d, 4))) for d in (1, 2, 3)]
    rs(groups[0], 4)
    for k in steps:
        k.wait()
    r.total[...] = r.sums[...] + r.sum_in[3] + r.sum_in[4] + r.sum_in[5]
    own_rows(zdu, r.gin, 3, False, True)
    rows_back_wait(zdu, r.gin, 3)
    rows_out(r.x_own, x_ref, 0, True)
    rows_out(r.dy_own, dy, 1, True)


def run_kernel(comm, x, dy, weights, vectors, biases):
    vmem, hbm = pl.BlockSpec(memory_space=pltpu.VMEM), pl.BlockSpec(memory_space=pl.ANY)
    units, own = (UNITS, ROWS, WIDTH), (x.shape[0], ROWS, WIDTH)
    shape = jax.ShapeDtypeStruct
    sem = pltpu.SemaphoreType.DMA
    ins = ["x_own", "dy_own", "wsh" if comm else "g_in", "vec", "bsh" if comm else "bz"]
    in_specs = [hbm, hbm, vmem if comm else hbm, vmem, vmem]
    outs = {"yout": (shape(own, BF16), hbm), "gin": (shape(own, BF16), hbm)}
    if comm:
        outs |= {"gsh": (shape((96, COLS), F32), vmem), "total": (shape((16, WIDTH), F32), vmem)}
    else:
        outs |= {"gout": (shape((4, 2, 2, 2, 96, COLS), BF16), hbm), "sums": (shape((16, WIDTH), F32), vmem)}
    scratch = {
        "g": pltpu.VMEM((4, 2, 2, 2, 96, COLS), BF16),
        "wb": pltpu.VMEM((WIDTH, 1536), BF16),
        "x": pltpu.VMEM(units, BF16),
        "qkv": pltpu.VMEM((UNITS, ROWS, COLS), BF16),
        "att": pltpu.VMEM(units, BF16),
        "h2": pltpu.VMEM(units, BF16),
        "dy": pltpu.VMEM(units, BF16),
        "y": pltpu.VMEM(units, F32),
        "e": pltpu.VMEM(units, F32),
        "lse": pltpu.VMEM((UNITS, ROWS, 128), F32),
        "zdu": pltpu.VMEM((UNITS, ROWS, 1024), BF16),
        "terms": pltpu.VMEM((UNITS, ROWS, 128), BF16),
        "pad": pltpu.VMEM((4 * ROWS, 128), BF16),
        "six": pltpu.VMEM((6, 8, 512), F32),
        "loc_sem": sem((4, 5)),
    }
    if comm:
        scratch |= {
            "sums": pltpu.VMEM((16, WIDTH), F32),
            "sum_in": pltpu.VMEM((6, 16, WIDTH), F32),
            "bz": pltpu.VMEM((4, 8, WIDTH), F32),
            "rc": pltpu.VMEM((2, 4, 2, 2, 96, 512), BF16),
            "r2": pltpu.VMEM((2, 2, 4, 2, 48, 512), BF16),
            "r1": pltpu.VMEM((2, 2, 4, 48, 512), BF16),
            "rz": pltpu.VMEM((2, 3, 96, 512), BF16),
            "ag_send": sem((5, 8)), "ag_recv": sem((5, 8)),
            "rs_send": sem((5, 8)), "rs_recv": sem((5, 8)),
            "row_send": sem((4, 3)), "row_recv": sem((4, 3)),
            "bias_send": sem((3,)), "bias_recv": sem((3,)),
            "sum_send": sem((6,)), "sum_recv": sem((6,)),
        }
    params = dict(collective_id=0, has_side_effects=True) if comm else {}
    return pl.pallas_call(
        functools.partial(kernel, ins + list(outs) + list(scratch), comm),
        out_shape=[v[0] for v in outs.values()],
        in_specs=in_specs,
        out_specs=[v[1] for v in outs.values()],
        scratch_shapes=list(scratch.values()),
        compiler_params=pltpu.CompilerParams(vmem_limit_bytes=64 * 2**20 - 2**16, **params),
    )(x, dy, weights, vectors, biases)


def pack_shard(attention_in, attention_out, hidden_in, hidden_out):
    q, k, v = attention_in[:, 0] * 0.125, attention_in[:, 1], attention_in[:, 2]
    out_t, down_t = attention_out.T, hidden_out.T
    cols = [q[:, :128], k[:, :128], v[:, :128], out_t[:, :128], q[:, 128:], k[:, 128:], v[:, 128:], out_t[:, 128:]]
    for c in range(CHUNKS):
        cols += [hidden_in[:, 256 * c : 256 * (c + 1)], down_t[:, 256 * c : 256 * (c + 1)]]
    return jnp.concatenate([t.astype(BF16) for t in cols], axis=1)


def unpack_shard(grad):
    q = jnp.concatenate([grad[:, 0:128], grad[:, 512:576]], axis=1) * 0.125
    k = jnp.concatenate([grad[:, 128:256], grad[:, 576:640]], axis=1)
    v = jnp.concatenate([grad[:, 256:384], grad[:, 640:704]], axis=1)
    out_t = jnp.concatenate([grad[:, 384:512], grad[:, 704:768]], axis=1)
    up = jnp.concatenate([grad[:, 768 + 512 * c : 1024 + 512 * c] for c in range(CHUNKS)], axis=1)
    down = jnp.concatenate([grad[:, 1024 + 512 * c : 1280 + 512 * c] for c in range(CHUNKS)], axis=1)
    return jnp.stack([q, k, v], axis=1), out_t.T, up, down.T


def nesterov(weight_old, moment_old, average_old, gradient, rate, decay):
    step_dir = gradient + decay * weight_old
    moment_new = MOMENTUM * moment_old + step_dir
    weight_new = weight_old - rate * (step_dir + MOMENTUM * moment_new)
    return (weight_new, moment_new, AVERAGE * average_old + (1.0 - AVERAGE) * weight_new)


def local(
    tokens, cotangent, slot_live,
    vectors, vectors_momentum, vectors_average,
    column_bias, column_bias_momentum, column_bias_average,
    hidden_bias, hidden_bias_momentum, hidden_bias_average,
    attention_in, attention_in_momentum, attention_in_average,
    attention_out, attention_out_momentum, attention_out_average,
    hidden_in, hidden_in_momentum, hidden_in_average,
    hidden_out, hidden_out_momentum, hidden_out_average,
):
    rows_dev = tokens.shape[0]
    rank = lax.axis_index("mp")
    total_rows = rows_dev * lax.axis_size("mp") * lax.axis_size("dp")
    own_units = rows_dev // UNIT
    unit = rank * own_units + jnp.arange(own_units, dtype=jnp.int32)
    slot = jnp.where(unit < 4 * SLOT_L, unit // 4, unit - 3 * SLOT_L)
    live = jnp.sum(
        jnp.where(slot[:, None] == jnp.arange(slot_live.shape[1], dtype=jnp.int32)[None], slot_live, 0), axis=1
    ).astype(BF16)

    def in_units(rows):
        return jnp.pad(rows.reshape(own_units, UNIT, WIDTH), ((0, 0), (0, ROWS - UNIT), (0, 0)))

    def take(units, table):
        return jnp.take(units, jnp.array(table, jnp.int32)[rank], axis=0)

    def to_work(units):
        got = lax.ppermute(units[3:5], "mp", [(0, 1), (1, 2), (2, 3)])
        table = [[0, 1, 2, 3, 3, 3, 3], [0, 1, 2, 6, 6, 6, 6], [0, 1, 5, 6, 2, 2, 2], [0, 1, 2, 3, 4, 5, 6]]
        return take(jnp.concatenate([units, got], axis=0), table)

    def from_work(work):
        theirs = take(work, [[0, 0], [3, 3], [2, 3], [5, 6]])
        got = lax.ppermute(theirs, "mp", [(1, 0), (2, 1), (3, 2)])
        table = [[0, 1, 2, 3, 8], [0, 1, 2, 7, 8], [0, 1, 4, 7, 8], [0, 1, 2, 3, 4]]
        return take(jnp.concatenate([work, got], axis=0), table)[:, :UNIT].reshape(rows_dev, WIDTH)

    x, dy = in_units(tokens), in_units(cotangent) * live[:, None, None]
    shard = pack_shard(attention_in, attention_out, hidden_in, hidden_out)
    bq, bv = column_bias[0] * 0.125, column_bias[1]
    none = jnp.zeros((128,), F32)
    row = jnp.concatenate([bq[:128], none, bv[:128], bq[128:], none[:64], bv[128:], none, none[:64]])
    bias_rows = jnp.concatenate([hidden_bias[None], row[None], jnp.zeros((6, WIDTH), F32)], axis=0)

    if lax.axis_size("dp") == 8:
        yout, gin, reduced, total = run_kernel(True, x, dy, shard, vectors, bias_rows)
        block_output, input_gradient = (t[:, :UNIT].reshape(rows_dev, WIDTH) for t in (yout, gin))
    else:
        weights = lax.all_gather(lax.all_gather(shard, "dp", axis=0, tiled=True), "mp", axis=0)
        weights = weights.reshape(4, 2, 2, 2, 96, COLS)
        all_bias = lax.all_gather(bias_rows, "mp", axis=0)
        yout, gin, grads, total = run_kernel(False, to_work(x), to_work(dy), weights, vectors, all_bias)
        block_output, input_gradient = from_work(yout), from_work(gin)
        reduced = lax.psum_scatter(grads.reshape(4, WIDTH, COLS), "mp", scatter_dimension=0, tiled=True)[0]
        reduced = lax.psum_scatter(reduced, "dp", scatter_dimension=0, tiled=True).astype(F32)
        total = lax.psum(total, ("dp", "mp"))
    vector_grad = total[0:6]
    hidden_grad = jnp.transpose(total[6:10].reshape(CHUNKS, 2, 2, 256), (1, 2, 0, 3)).reshape(4, 768)
    hidden_grad = lax.dynamic_index_in_dim(hidden_grad, rank, 0, keepdims=False)
    pq, pv = total[10].reshape(PAIRS, 2, 64), total[11].reshape(PAIRS, 2, 64)

    def own_heads(pairs):
        second = pairs[4:6].reshape(4, 64)
        return jnp.concatenate(
            [lax.dynamic_index_in_dim(pairs, rank, 0, keepdims=False).reshape(128),
             lax.dynamic_index_in_dim(second, rank, 0, keepdims=False)]
        )

    column_grad = jnp.stack([own_heads(pq) * 0.125, own_heads(pv)])
    gqkv, gout, gup, gdown = unpack_shard(reduced)
    root = math.sqrt(total_rows)
    steps = (
        (vectors, vectors_momentum, vectors_average, vector_grad, RATE_VECTORS, 0.0),
        (column_bias, column_bias_momentum, column_bias_average, column_grad, RATE_COLUMN, 0.0),
        (hidden_bias, hidden_bias_momentum, hidden_bias_average, hidden_grad, RATE_HIDDEN, 0.0),
        (attention_in, attention_in_momentum, attention_in_average, gqkv, RATE_ATTENTION_IN, DECAY),
        (attention_out, attention_out_momentum, attention_out_average, gout, RATE_ATTENTION_OUT, DECAY),
        (hidden_in, hidden_in_momentum, hidden_in_average, gup, RATE_HIDDEN_IN, DECAY),
        (hidden_out, hidden_out_momentum, hidden_out_average, gdown, RATE_HIDDEN_OUT, DECAY),
    )
    outs = [block_output, input_gradient]
    for weight, moment, average, gradient, rate, decay in steps:
        outs.extend(nesterov(weight, moment, average, gradient, rate / root, decay))
    return tuple(outs)


def solution(mesh):
    rows, matrix, side = P(("dp", "mp"), None), P("dp", None, "mp"), P("mp", "dp")
    params = [P()] * 3 + [P(None, "mp")] * 3 + [P("mp")] * 3 + [matrix] * 3 + [side] * 3 + [P("dp", "mp")] * 3 + [side] * 3
    return jax.shard_map(
        local,
        mesh=mesh,
        in_specs=(rows, rows, P("dp", None), *params),
        out_specs=(rows, rows, *params),
        check_vma=False,
    )
```
